32 devices in a mesh: pipe: 4 (over y, x), seq: 8 (over z, core).
Axes of the slice: x: 2, y: 2, z: 4, core: 2. Of those that a mesh axis runs over, the one named last changes fastest.
Arguments:
- query_rows: bfloat16 [4, 1024, 1536], P('pipe', 'seq'), may hold values from -6 to 6
- key_rows: bfloat16 [4, 1024, 1536], P('pipe', 'seq'), may hold values from -6 to 6
- value_rows: bfloat16 [4, 1024, 1536], P('pipe', 'seq'), may hold values from -6 to 6
- query_weight: bfloat16 [4, 1536, 1536], P('pipe'), may hold values from -0.15625 to 0.15625
- key_weight: bfloat16 [4, 1536, 1536], P('pipe'), may hold values from -0.15625 to 0.15625
- value_weight: bfloat16 [4, 1536, 1536], P('pipe'), may hold values from -0.15625 to 0.15625
- out_weight: bfloat16 [4, 1536, 1536], P('pipe'), may hold values from -0.15625 to 0.15625
- upstream: bfloat16 [1024, 1536], P('seq'), may hold values from -6 to 6
- window: int32 [8, 12, 2], replicated, may hold values from 0 to 1, as said below
Outputs:
- gradients: bfloat16 [4, 1024, 1536], P('pipe', 'seq')
The draws below stay inside these ranges and needn't reach their ends.
Inputs may be any that keep to these rules, and one draw needn't show every extreme that they name: window[i, h, 0] is 0 where i % 4 == 3, and window[i, h, 1] is 0 where i % 4 == 2.
All inputs are finite; a program needn't handle non-finite values.
Results may differ from the reference program's by a relative error of at most 0.02.
Values may be sent and summed in bfloat16 or wider, within the bound.
No kernel may reach another device: no remote copies, remote signals or barrier semaphores. Data moves between devices by JAX's collectives and lax.ppermute only.
A program may use at most 128 MiB of HBM per device.

```python
import jax
import jax.numpy as jnp
from jax import lax

D = 1536
HEADS = 12
HEAD_DIM = 128
TILE = 128
COLUMN = 4
SECTIONS = 4
TILES = 8
TOKENS = 1024
HW = 1536


def draw_query_rows(key, part):
    shape = (SECTIONS, TOKENS, HEADS, HEAD_DIM)
    base = jnp.clip(1.4 * jax.random.normal(jax.random.fold_in(key, 1), shape, jnp.float32), -6.0, 6.0)
    return base.reshape(SECTIONS, TOKENS, HEADS * HEAD_DIM).astype(jnp.bfloat16)


def draw_key_rows(key, part):
    shape = (SECTIONS, TOKENS, HEADS, HEAD_DIM)
    base = jnp.clip(1.4 * jax.random.normal(jax.random.fold_in(key, 2), shape, jnp.float32), -6.0, 6.0)
    return base.reshape(SECTIONS, TOKENS, HEADS * HEAD_DIM).astype(jnp.bfloat16)


def draw_window(key, part):
    level = jax.random.randint(jax.random.fold_in(key, 21), (TILES, 1, 1), 0, 4)
    picks = jax.random.randint(jax.random.fold_in(key, 22), (TILES, HEADS, 2), 0, 3)
    flags = (picks < level).astype(jnp.int32)
    chosen = jax.random.randint(jax.random.fold_in(key, 23), (TILES, 1, 1), 0, HEADS)
    heads = jnp.arange(HEADS)[None, :, None]
    flags = jnp.where(heads == chosen, 1, flags)
    places = jnp.arange(TILES) % COLUMN
    side_before = jnp.where((places == COLUMN - 1)[:, None], 0, flags[:, :, 0])
    side_after = jnp.where((places == COLUMN - 2)[:, None], 0, flags[:, :, 1])
    return jnp.stack([side_before, side_after], axis=-1).astype(jnp.int32)


def level_of(rng, extent, shards, least, largest):
    def one(position, blocks):
        heights = jax.random.uniform(jax.random.fold_in(jax.random.fold_in(rng, 6), position), (blocks,), jnp.float32, least / len(shards), largest / len(shards))
        return jnp.repeat(jnp.exp(heights), extent[position] // blocks).reshape((-1,) + (1,) * (len(extent) - position - 1))

    factor_of = one(*shards[0])
    for cut in shards[1:]:
        factor_of = factor_of * one(*cut)
    return factor_of


def normal_values(key, dims, scale, reach, cuts=(), kind=jnp.bfloat16):
    drawn = jax.random.normal(key, dims, jnp.float32) * scale
    if len(cuts) > 0:
        drawn = level_of(key, dims, cuts, -0.22, 0.18) * drawn
    return jnp.clip(drawn, min=-reach, max=reach).astype(kind)


def setup_inputs(seed: int = 0) -> dict:
    keys = jax.random.split(jax.random.key(seed), 10)
    query_rows = draw_query_rows(jax.random.fold_in(keys[9], 71), 0)
    key_rows = draw_key_rows(jax.random.fold_in(keys[9], 71), 0)
    value_rows = normal_values(keys[2], (SECTIONS, TOKENS, HW), 1.0, 6.0, ((0, 4), (1, 8)))
    query_weight = normal_values(keys[3], (SECTIONS, D, HW), HW ** -0.5, 0.15625, ((0, 4),))
    key_weight = normal_values(keys[4], (SECTIONS, D, HW), HW ** -0.5, 0.15625, ((0, 4),))
    value_weight = normal_values(keys[5], (SECTIONS, D, HW), HW ** -0.5, 0.15625, ((0, 4),))
    out_weight = normal_values(keys[6], (SECTIONS, HW, D), D ** -0.5, 0.15625, ((0, 4),))
    upstream = normal_values(keys[7], (TOKENS, D), 1.0, 6.0, ((0, 8),))
    window = draw_window(jax.random.fold_in(keys[9], 71), 0)
    return {"query_rows": query_rows, "key_rows": key_rows, "value_rows": value_rows, "query_weight": query_weight, "key_weight": key_weight, "value_weight": value_weight, "out_weight": out_weight, "upstream": upstream, "window": window}


def contract_last(first_operand, second_operand):
    return lax.dot_general(first_operand, second_operand, (((1,), (1,)), ((), ())), preferred_element_type=jnp.float32)


def combine_parts(partials):
    empty_tile = jnp.zeros_like(partials[:1, 0])
    from_next = jnp.concatenate([partials[1:, 0], empty_tile], 0)
    from_prev = jnp.concatenate([empty_tile, partials[:-1, 2]], 0)
    return (partials[:, 1] + from_next + from_prev).astype(jnp.bfloat16).reshape(TOKENS, HW)


def section_backward(incoming, query_matrix, key_matrix, value_matrix, out_matrix, queries_all, keys_all, values_all, window):
    scaling = HEAD_DIM ** -0.5
    d_out = contract_last(incoming, out_matrix).astype(jnp.bfloat16)
    tile_shape = (TILES, TILE, HEADS, HEAD_DIM)
    query_tiles = queries_all.reshape(tile_shape)
    out_tiles = d_out.reshape(tile_shape)
    padding = ((1, 1), (0, 0), (0, 0), (0, 0))
    key_padded = jnp.pad(keys_all.reshape(tile_shape), padding)
    value_padded = jnp.pad(values_all.reshape(tile_shape), padding)
    block_shape = (3, TILE, HEADS, HEAD_DIM)

    def one_tile(tile_index):
        tile_index = tile_index.astype(jnp.int32)
        queries = query_tiles[tile_index].astype(jnp.float32)
        grads_out = out_tiles[tile_index].astype(jnp.float32)
        anchor = (tile_index, jnp.int32(0), jnp.int32(0), jnp.int32(0))
        key_block = lax.dynamic_slice(key_padded, anchor, block_shape).reshape(3 * TILE, HEADS, HEAD_DIM).astype(jnp.float32)
        value_block = lax.dynamic_slice(value_padded, anchor, block_shape).reshape(3 * TILE, HEADS, HEAD_DIM).astype(jnp.float32)
        side_flags = window[tile_index] > 0
        keep_mask = jnp.concatenate([jnp.repeat(side_flags[:, 0:1], TILE, axis=1), jnp.ones((HEADS, TILE), dtype=bool), jnp.repeat(side_flags[:, 1:2], TILE, axis=1)], axis=1)
        scores = scaling * jnp.einsum("qhd,khd->hqk", queries, key_block)
        scores = jnp.where(keep_mask[:, None, :], scores, -jnp.inf)
        row_max = jnp.max(scores, axis=-1, keepdims=True)
        log_total = row_max + jnp.log(jnp.sum(jnp.exp(scores - row_max), axis=-1, keepdims=True))
        weights = jnp.exp(scores - log_total)
        weight_change = jnp.einsum("qhd,khd->hqk", grads_out, value_block)
        row_delta = jnp.sum(weights * weight_change, axis=-1, keepdims=True)
        score_change = lax.optimization_barrier((weights * (weight_change - row_delta)).astype(jnp.bfloat16)).astype(jnp.float32)
        weights_low = lax.optimization_barrier(weights.astype(jnp.bfloat16)).astype(jnp.float32)
        query_gradient = (scaling * jnp.einsum("hqk,khd->qhd", score_change, key_block)).astype(jnp.bfloat16)
        key_part = scaling * jnp.einsum("hqk,qhd->khd", score_change, queries)
        value_part = jnp.einsum("hqk,qhd->khd", weights_low, grads_out)
        return query_gradient.reshape(TILE, HW), key_part.reshape(3, TILE, HW), value_part.reshape(3, TILE, HW)

    query_parts, key_parts, value_parts = lax.map(one_tile, jnp.arange(TILES, dtype=jnp.int32))
    query_gradient = query_parts.reshape(TOKENS, HW)
    key_gradient = combine_parts(key_parts)
    value_gradient = combine_parts(value_parts)
    total = incoming.astype(jnp.float32) + contract_last(query_gradient, query_matrix)
    total = total + contract_last(key_gradient, key_matrix) + contract_last(value_gradient, value_matrix)
    return total.astype(jnp.bfloat16)


def reference(query_rows, key_rows, value_rows, query_weight, key_weight, value_weight, out_weight, upstream, window):
    incoming = upstream
    results = []
    for section_index in range(SECTIONS - 1, -1, -1):
        incoming = section_backward(incoming, query_weight[section_index], key_weight[section_index], value_weight[section_index], out_weight[section_index], query_rows[section_index], key_rows[section_index], value_rows[section_index], window)
        results.append(incoming)
    return jnp.stack(results[::-1])
```

```python
import functools

import jax
import jax.numpy as jnp
from jax import lax
from jax.experimental import pallas as pl
from jax.experimental.pallas import tpu as pltpu
from jax.sharding import PartitionSpec as P

HEAD_DIM = 128
TILE = 128
MIB = 1 << 20


def dot_nt(a, b):
    return lax.dot_general(a, b, (((1,), (1,)), ((), ())), preferred_element_type=jnp.float32)


def dot_nn(a, b):
    return lax.dot_general(a, b, (((1,), (0,)), ((), ())), preferred_element_type=jnp.float32)


def prob_kernel(heads, scaling, flags, q_ref, k0_ref, k1_ref, k2_ref, pt_ref, kt_ref):
    for h in range(heads):
        cols = pl.ds(h * HEAD_DIM, HEAD_DIM)
        q = q_ref[:, cols]
        scores = []
        for b, k_ref in enumerate((k0_ref, k1_ref, k2_ref)):
            k = k_ref[:, cols]
            s = scaling * dot_nt(k, q)
            if b > 0:
                s = jnp.where(flags[b - 1, h] > 0, s, -jnp.inf)
            scores.append(s)
            kt_ref[h, :, pl.ds(b * TILE, TILE)] = k.T
        top = jnp.maximum(jnp.maximum(scores[0], scores[1]), scores[2])
        top = jnp.max(top, axis=0, keepdims=True)
        weights = [jnp.exp(s - top) for s in scores]
        total = jnp.sum(weights[0] + weights[1] + weights[2], axis=0, keepdims=True)
        scale = 1.0 / total
        for b, w in enumerate(weights):
            pt_ref[h, pl.ds(b * TILE, TILE), :] = (w * scale).astype(jnp.bfloat16)


def stage_kernel(
    heads,
    scaling,
    x_ref,
    q_ref,
    v0_ref,
    v1_ref,
    v2_ref,
    pt_ref,
    kt_ref,
    wo_hbm,
    wq_hbm,
    wk_hbm,
    wv_hbm,
    own_ref,
    core_ref,
    far_ref,
    wo,
    wq,
    wk,
    wv,
    dq,
    dk,
    dv,
    sems,
):
    width = wo.shape[0]
    groups = 4
    rows = width // groups
    out_copies = []
    for g in range(groups):
        part = pl.ds(g * rows, rows)
        out_copies.append(pltpu.make_async_copy(wo_hbm.at[part], wo.at[part], sems.at[g]))
    others = [
        pltpu.make_async_copy(src, dst, sems.at[groups + n])
        for n, (src, dst) in enumerate(((wk_hbm, wk), (wv_hbm, wv), (wq_hbm, wq)))
    ]
    for copy in out_copies + others:
        copy.start()
    x = x_ref[...]
    per = heads // groups
    for g in range(groups):
        out_copies[g].wait()
        d_out = dot_nt(x, wo[pl.ds(g * rows, rows), :]).astype(jnp.bfloat16)
        for n in range(per):
            h = g * per + n
            cols = pl.ds(h * HEAD_DIM, HEAD_DIM)
            dh = d_out[:, n * HEAD_DIM : (n + 1) * HEAD_DIM]
            p = [pt_ref[h, pl.ds(b * TILE, TILE), :] for b in range(3)]
            pf = [t.astype(jnp.float32) for t in p]
            dp = [dot_nt(v_ref[:, cols], dh) for v_ref in (v0_ref, v1_ref, v2_ref)]
            prod = [a * b for a, b in zip(pf, dp)]
            delta = jnp.sum(prod[0] + prod[1] + prod[2], axis=0, keepdims=True)
            ds = [(a * ((b - delta) * scaling)).astype(jnp.bfloat16) for a, b in zip(pf, dp)]
            ds_all = jnp.concatenate(ds, axis=0)
            dq_t = dot_nn(kt_ref[h], ds_all)
            dq[:, cols] = dq_t.T.astype(jnp.bfloat16)
            dk[:, cols] = dot_nn(ds_all, q_ref[:, cols]).astype(jnp.bfloat16)
            dv[:, cols] = dot_nn(pt_ref[h], dh).astype(jnp.bfloat16)
    for copy in others:
        copy.wait()
    step = 512
    for n in range(own_ref.shape[1] // step):
        part = pl.ds(n * step, step)
        cross = dot_nt(dk[...], wk[part, :]) + dot_nt(dv[...], wv[part, :])
        own = cross[:TILE] + dot_nt(dq[...], wq[part, :]) + x_ref[:, part].astype(jnp.float32)
        own_ref[:, part] = own
        core_ref[:, part] = cross[TILE : 2 * TILE].astype(jnp.bfloat16)
        far_ref[:, part] = cross[2 * TILE :].astype(jnp.bfloat16)


def body(
    query_rows,
    key_rows,
    value_rows,
    query_weight,
    key_weight,
    value_weight,
    out_weight,
    upstream,
    window,
):
    sections = lax.axis_size("pipe")
    position = lax.axis_index("pipe")
    seq_size = lax.axis_size("seq")
    seq_index = lax.axis_index("seq")
    rows, width = query_rows.shape[1:]
    model = out_weight.shape[2]
    heads = width // HEAD_DIM
    scaling = HEAD_DIM ** (-0.5)
    near_pairs = [(i, i ^ 1) for i in range(seq_size)]
    far_pairs = [(i, i + 1) for i in range(1, seq_size - 1, 2)]
    far_pairs = far_pairs + [(j, i) for i, j in far_pairs]

    def near(value):
        return lax.ppermute(value, "seq", near_pairs)

    def far(value):
        return lax.ppermute(value, "seq", far_pairs)

    q, k, v = query_rows[0], key_rows[0], value_rows[0]
    k1, k2 = near(k), far(k)
    v1, v2 = near(v), far(v)
    flags = lax.dynamic_index_in_dim(window, seq_index, 0, keepdims=False)
    odd = seq_index % 2 == 1
    flags = jnp.where(
        odd,
        jnp.stack([flags[:, 0], flags[:, 1]]),
        jnp.stack([flags[:, 1], flags[:, 0]]),
    )
    vmem = pl.BlockSpec(memory_space=pltpu.VMEM)
    smem = pl.BlockSpec(memory_space=pltpu.SMEM)
    anywhere = pl.BlockSpec(memory_space=pl.ANY)
    bf16 = jnp.bfloat16
    pt, kt = pl.pallas_call(
        functools.partial(prob_kernel, heads, scaling),
        in_specs=[smem, vmem, vmem, vmem, vmem],
        out_specs=[vmem, vmem],
        out_shape=[
            jax.ShapeDtypeStruct((heads, 3 * TILE, rows), bf16),
            jax.ShapeDtypeStruct((heads, HEAD_DIM, 3 * TILE), bf16),
        ],
        compiler_params=pltpu.CompilerParams(vmem_limit_bytes=32 * MIB),
        name="prob",
    )(flags, q, k, k1, k2)

    stage = pl.pallas_call(
        functools.partial(stage_kernel, heads, scaling),
        in_specs=[vmem] * 7 + [anywhere] * 4,
        out_specs=[vmem] * 3,
        out_shape=[
            jax.ShapeDtypeStruct((rows, model), jnp.float32),
            jax.ShapeDtypeStruct((rows, model), bf16),
            jax.ShapeDtypeStruct((rows, model), bf16),
        ],
        scratch_shapes=[
            pltpu.VMEM((width, model), bf16),
            pltpu.VMEM((model, width), bf16),
            pltpu.VMEM((model, width), bf16),
            pltpu.VMEM((model, width), bf16),
            pltpu.VMEM((rows, width), bf16),
            pltpu.VMEM((3 * rows, width), bf16),
            pltpu.VMEM((3 * rows, width), bf16),
            pltpu.SemaphoreType.DMA((7,)),
        ],
        compiler_params=pltpu.CompilerParams(vmem_limit_bytes=48 * MIB),
        name="stage",
    )
    wo, wq, wk, wv = out_weight[0], query_weight[0], key_weight[0], value_weight[0]
    incoming = upstream
    result = jnp.zeros((rows, model), bf16)
    for step in range(sections):
        own, to_near, to_far = stage(incoming, q, v, v1, v2, pt, kt, wo, wq, wk, wv)
        from_far = far(to_far)
        from_near = near(to_near)
        finished = own + from_near.astype(jnp.float32) + from_far.astype(jnp.float32)
        finished = finished.astype(bf16)
        result = jnp.where(position == sections - 1 - step, finished, result)
        if step < sections - 1:
            source = sections - 1 - step
            incoming = lax.ppermute(finished, "pipe", [(source, source - 1)])
    return result[None]


def solution(mesh):
    in_specs = (
        P("pipe", "seq", None),
        P("pipe", "seq", None),
        P("pipe", "seq", None),
        P("pipe", None, None),
        P("pipe", None, None),
        P("pipe", None, None),
        P("pipe", None, None),
        P("seq", None),
        P(),
    )
    out_specs = P("pipe", "seq", None)
    return jax.shard_map(body, mesh=mesh, in_specs=in_specs, out_specs=out_specs, check_vma=False)
```

```python
import functools

import jax
import jax.numpy as jnp
from jax import lax
from jax.experimental import pallas as pl
from jax.experimental.pallas import tpu as pltpu
from jax.sharding import PartitionSpec as P

HEAD_DIM = 128
TILE = 128
MIB = 1 << 20


def dot_nt(a, b):
    return lax.dot_general(a, b, (((1,), (1,)), ((), ())), preferred_element_type=jnp.float32)


def dot_nn(a, b):
    return lax.dot_general(a, b, (((1,), (0,)), ((), ())), preferred_element_type=jnp.float32)


def pair_cols(g):
    return pl.ds(g * 2 * HEAD_DIM, 2 * HEAD_DIM)


def put_diagonal(target, g, value):
    target[g, pl.ds(0, TILE), pl.ds(0, HEAD_DIM)] = value[:, :HEAD_DIM]
    target[g, pl.ds(TILE, TILE), pl.ds(HEAD_DIM, HEAD_DIM)] = value[:, HEAD_DIM:]


def prep_kernel(
    wo_hbm, wq_hbm, wk_hbm, wv_hbm, q_hbm, k_hbm, v_hbm, wot, wq, wk, wv, q, k, v, qbd, wo, sems
):
    groups = 4
    rows = wo.shape[0] // groups
    small = [
        pltpu.make_async_copy(src, dst, sems.at[n])
        for n, (src, dst) in enumerate(((k_hbm, k), (q_hbm, q), (v_hbm, v)))
    ]
    out_copies = []
    for g in range(groups):
        part = pl.ds(g * rows, rows)
        out_copies.append(pltpu.make_async_copy(wo_hbm.at[part], wo.at[part], sems.at[3 + g]))
    others = [
        pltpu.make_async_copy(src, dst, sems.at[3 + groups + n])
        for n, (src, dst) in enumerate(((wk_hbm, wk), (wv_hbm, wv), (wq_hbm, wq)))
    ]
    for copy in small + out_copies + others:
        copy.start()
    qbd[...] = jnp.zeros_like(qbd)
    for copy in small:
        copy.wait()
    for g in range(qbd.shape[0]):
        put_diagonal(qbd, g, q[:, pair_cols(g)])
    for g in range(groups):
        out_copies[g].wait()
        for r in range(0, rows, TILE):
            part = pl.ds(g * rows + r, TILE)
            wot[:, part] = wo[part, :].T
    for copy in others:
        copy.wait()


def prob_kernel(scaling, window, q_ref, k0_ref, k1_ref, k2_ref, pt_ref, kt_ref):
    tile = lax.axis_index("seq")
    odd = lax.rem(tile, 2)
    for g in range(pt_ref.shape[0]):
        for n in range(2):
            h = 2 * g + n
            cols = pl.ds(h * HEAD_DIM, HEAD_DIM)
            q = q_ref[:, cols]
            scores = []
            for b, k_ref in enumerate((k0_ref, k1_ref, k2_ref)):
                k = k_ref[:, cols]
                s = scaling * dot_nt(k, q)
                if b > 0:
                    side = 1 - odd if b == 1 else odd
                    s = jnp.where(window[tile, side, h] > 0, s, -jnp.inf)
                scores.append(s)
                kt_ref[h, :, pl.ds(b * TILE, TILE)] = k.T
            top = jnp.maximum(jnp.maximum(scores[0], scores[1]), scores[2])
            top = jnp.max(top, axis=0, keepdims=True)
            weights = [jnp.exp(s - top) for s in scores]
            total = jnp.sum(weights[0] + weights[1] + weights[2], axis=0, keepdims=True)
            scale = 1.0 / total
            for b, w in enumerate(weights):
                pt_ref[g, pl.ds(b * TILE, TILE), pl.ds(n * TILE, TILE)] = (w * scale).astype(
                    jnp.bfloat16
                )


def cross_kernel(
    scaling, x_ref, wot, qbd, pt, v0, v1, v2, wk, wv, near_ref, far_ref, ds_ref, bd, dk, dv
):
    pairs = pt.shape[0]
    bd[...] = jnp.zeros_like(bd)
    x = x_ref[...]
    for g in range(pairs):
        cols = pair_cols(g)
        put_diagonal(bd, g, dot_nn(x, wot[:, cols]).astype(jnp.bfloat16))
    for g in range(pairs):
        cols = pair_cols(g)
        out = bd[g]
        p = pt[g]
        pf = p.astype(jnp.float32)
        values = jnp.concatenate([v0[:, cols], v1[:, cols], v2[:, cols]], axis=0)
        dp = dot_nt(values, out)
        delta = jnp.sum(pf * dp, axis=0, keepdims=True)
        ds = (pf * ((dp - delta) * scaling)).astype(jnp.bfloat16)
        ds_ref[g] = ds
        dv[:, cols] = dot_nn(p[TILE:], out).astype(jnp.bfloat16)
        dk[:, cols] = dot_nn(ds[TILE:], qbd[g]).astype(jnp.bfloat16)
    step = 768
    for n in range(near_ref.shape[1] // step):
        part = pl.ds(n * step, step)
        cross = dot_nt(dk[...], wk[part, :]) + dot_nt(dv[...], wv[part, :])
        cross = cross.astype(jnp.bfloat16)
        near_ref[:, part] = cross[:TILE]
        far_ref[:, part] = cross[TILE:]


def own_kernel(x_ref, ds_ref, bd, qbd, pt, kt, wq, wk, wv, own_ref, dq, dk, dv):
    for g in range(pt.shape[0]):
        cols = pair_cols(g)
        ds = ds_ref[g]
        dv[:, cols] = dot_nn(pt[g, :TILE], bd[g]).astype(jnp.bfloat16)
        dk[:, cols] = dot_nn(ds[:TILE], qbd[g]).astype(jnp.bfloat16)
        for n in range(2):
            h = 2 * g + n
            dq_t = dot_nn(kt[h], ds[:, n * TILE : (n + 1) * TILE])
            dq[:, pl.ds(h * HEAD_DIM, HEAD_DIM)] = dq_t.T.astype(jnp.bfloat16)
    step = 768
    for n in range(own_ref.shape[1] // step):
        part = pl.ds(n * step, step)
        own_ref[:, part] = (
            dot_nt(dq[...], wq[part, :])
            + dot_nt(dk[...], wk[part, :])
            + dot_nt(dv[...], wv[part, :])
            + x_ref[:, part].astype(jnp.float32)
        )


def sum_kernel(own_ref, near_ref, far_ref, sum_ref):
    total = own_ref[...] + near_ref[...].astype(jnp.float32) + far_ref[...].astype(jnp.float32)
    sum_ref[...] = total.astype(jnp.bfloat16)


def pick_kernel(*refs):
    done_refs, out_ref = refs[:-1], refs[-1]
    position = lax.axis_index("pipe")
    for step, done_ref in enumerate(done_refs):

        @pl.when(position == len(done_refs) - 1 - step)
        def _():
            out_ref[...] = done_ref[...]


def body(
    query_rows,
    key_rows,
    value_rows,
    query_weight,
    key_weight,
    value_weight,
    out_weight,
    upstream,
    window,
):
    sections = lax.axis_size("pipe")
    position = lax.axis_index("pipe")
    seq_size = lax.axis_size("seq")
    seq_index = lax.axis_index("seq")
    rows, width = query_rows.shape[1:]
    model = out_weight.shape[2]
    heads = width // HEAD_DIM
    pairs = heads // 2
    scaling = HEAD_DIM ** (-0.5)
    near_pairs = [(i, i ^ 1) for i in range(seq_size)]
    far_pairs = [(i, i + 1) for i in range(1, seq_size - 1, 2)]
    far_pairs = far_pairs + [(j, i) for i, j in far_pairs]

    def near(value):
        return lax.ppermute(value, "seq", near_pairs)

    def far(value):
        return lax.ppermute(value, "seq", far_pairs)

    k2 = far(key_rows[0])
    v2 = far(value_rows[0])
    k1 = near(key_rows[0])
    v1 = near(value_rows[0])
    vmem = pl.BlockSpec(memory_space=pltpu.VMEM)
    smem = pl.BlockSpec(memory_space=pltpu.SMEM)
    hbm = pl.BlockSpec(memory_space=pltpu.HBM)
    bf16 = jnp.bfloat16

    def params(mib):
        return pltpu.CompilerParams(vmem_limit_bytes=mib * MIB)

    wot, wq, wk, wv, q, k, v, qbd = pl.pallas_call(
        prep_kernel,
        in_specs=[hbm] * 7,
        out_specs=[vmem] * 8,
        out_shape=[
            pltpu.VMEM((model, width), bf16),
            pltpu.VMEM((model, width), bf16),
            pltpu.VMEM((model, width), bf16),
            pltpu.VMEM((model, width), bf16),
            pltpu.VMEM((rows, width), bf16),
            pltpu.VMEM((rows, width), bf16),
            pltpu.VMEM((rows, width), bf16),
            pltpu.VMEM((pairs, 2 * TILE, 2 * HEAD_DIM), bf16),
        ],
        scratch_shapes=[pltpu.VMEM((width, model), bf16), pltpu.SemaphoreType.DMA((10,))],
        compiler_params=params(36),
        name="prep",
    )(
        out_weight[0],
        query_weight[0],
        key_weight[0],
        value_weight[0],
        query_rows[0],
        key_rows[0],
        value_rows[0],
    )
    pt, kt = pl.pallas_call(
        functools.partial(prob_kernel, scaling),
        in_specs=[smem, vmem, vmem, vmem, vmem],
        out_specs=[vmem, vmem],
        out_shape=[
            pltpu.VMEM((pairs, 3 * TILE, 2 * rows), bf16),
            pltpu.VMEM((heads, HEAD_DIM, 3 * TILE), bf16),
        ],
        compiler_params=params(16),
        name="prob",
    )(jnp.transpose(window, (0, 2, 1)), q, k, k1, k2)

    cross = pl.pallas_call(
        functools.partial(cross_kernel, scaling),
        in_specs=[vmem] * 9,
        out_specs=[vmem] * 4,
        out_shape=[
            jax.ShapeDtypeStruct((rows, model), bf16),
            jax.ShapeDtypeStruct((rows, model), bf16),
            pltpu.VMEM((pairs, 3 * TILE, 2 * rows), bf16),
            pltpu.VMEM((pairs, 2 * TILE, 2 * HEAD_DIM), bf16),
        ],
        scratch_shapes=[
            pltpu.VMEM((2 * rows, width), bf16),
            pltpu.VMEM((2 * rows, width), bf16),
        ],
        compiler_params=params(16),
        name="cross",
    )
    own_call = pl.pallas_call(
        own_kernel,
        in_specs=[vmem] * 9,
        out_specs=vmem,
        out_shape=pltpu.VMEM((rows, model), jnp.float32),
        scratch_shapes=[pltpu.VMEM((rows, width), bf16)] * 3,
        compiler_params=params(16),
        name="own",
    )
    add_up = pl.pallas_call(
        sum_kernel,
        in_specs=[vmem] * 3,
        out_specs=vmem,
        out_shape=jax.ShapeDtypeStruct((rows, model), bf16),
        compiler_params=params(16),
        name="add_up",
    )
    pick = pl.pallas_call(
        pick_kernel,
        in_specs=[vmem] * sections,
        out_specs=vmem,
        out_shape=jax.ShapeDtypeStruct((rows, model), bf16),
        compiler_params=params(16),
        name="pick",
    )
    incoming = upstream
    done = []
    for step in range(sections):
        to_near, to_far, ds, bd = cross(incoming, wot, qbd, pt, v, v1, v2, wk, wv)
        from_far = far(to_far)
        from_near = near(to_near)
        own = own_call(incoming, ds, bd, qbd, pt, kt, wq, wk, wv)
        finished = add_up(own, from_near, from_far)
        done.append(finished)
        if step < sections - 1:
            source = sections - 1 - step
            incoming = lax.ppermute(finished, "pipe", [(source, source - 1)])
    return pick(*done)[None]


def solution(mesh):
    in_specs = (
        P("pipe", "seq", None),
        P("pipe", "seq", None),
        P("pipe", "seq", None),
        P("pipe", None, None),
        P("pipe", None, None),
        P("pipe", None, None),
        P("pipe", None, None),
        P("seq", None),
        P(),
    )
    out_specs = P("pipe", "seq", None)
    return jax.shard_map(body, mesh=mesh, in_specs=in_specs, out_specs=out_specs, check_vma=False)
```

```python
import functools

import jax
import jax.numpy as jnp
from jax import lax
from jax.experimental import pallas as pl
from jax.experimental.pallas import tpu as pltpu
from jax.sharding import PartitionSpec as P

HEAD_DIM = 128
TILE = 128
MIB = 1 << 20


def dot_nt(a, b):
    return lax.dot_general(a, b, (((1,), (1,)), ((), ())), preferred_element_type=jnp.float32)


def dot_nn(a, b):
    return lax.dot_general(a, b, (((1,), (0,)), ((), ())), preferred_element_type=jnp.float32)


def pair_cols(g):
    return pl.ds(g * 2 * HEAD_DIM, 2 * HEAD_DIM)


def put_diagonal(target, g, value):
    target[g, pl.ds(0, TILE), pl.ds(0, HEAD_DIM)] = value[:, :HEAD_DIM]
    target[g, pl.ds(TILE, TILE), pl.ds(HEAD_DIM, HEAD_DIM)] = value[:, HEAD_DIM:]


def prep_kernel(
    wo_hbm,
    wk_hbm,
    wv_hbm,
    wq_hbm,
    q_hbm,
    k_hbm,
    v_hbm,
    x_hbm,
    wot,
    wkt,
    wvt,
    wqt,
    q,
    k,
    v,
    x,
    qbd,
    raw,
    sems,
):
    groups = 4
    rows = raw.shape[1] // groups
    small = [
        pltpu.make_async_copy(src, dst, sems.at[n])
        for n, (src, dst) in enumerate(((q_hbm, q), (k_hbm, k), (v_hbm, v), (x_hbm, x)))
    ]
    large = []
    for n, src in enumerate((wo_hbm, wk_hbm, wv_hbm, wq_hbm)):
        for g in range(groups):
            part = pl.ds(g * rows, rows)
            sem = sems.at[4 + n * groups + g]
            large.append(pltpu.make_async_copy(src.at[part], raw.at[n, part], sem))
    for copy in small + large:
        copy.start()
    qbd[...] = jnp.zeros_like(qbd)
    for copy in small:
        copy.wait()
    for g in range(qbd.shape[0]):
        put_diagonal(qbd, g, q[:, pair_cols(g)])
    for n, dst in enumerate((wot, wkt, wvt, wqt)):
        for g in range(groups):
            large[n * groups + g].wait()
            for r in range(0, rows, TILE):
                part = pl.ds(g * rows + r, TILE)
                dst[:, part] = raw[n, part, :].T


def prob_kernel(scaling, window, qbd, k0, k1, k2, after, pt_ref, kt_ref, scores):
    pairs = pt_ref.shape[0]
    tile = lax.axis_index("seq")
    odd = lax.rem(tile, 2)
    for g in range(pairs):
        cols = pair_cols(g)
        keys = jnp.concatenate([k0[:, cols], k1[:, cols], k2[:, cols]], axis=0)
        scores[g] = dot_nt(keys, qbd[g])
        for b, k_ref in enumerate((k0, k1, k2)):
            for n in range(2):
                h = 2 * g + n
                part = k_ref[:, pl.ds(h * HEAD_DIM, HEAD_DIM)]
                kt_ref[h, :, pl.ds(b * TILE, TILE)] = part.T
    lane = lax.broadcasted_iota(jnp.int32, (TILE, 2 * TILE), 1)
    for g in range(pairs):
        parts = []
        for b in range(3):
            s = scaling * scores[g, pl.ds(b * TILE, TILE)]
            if b > 0:
                side = 1 - odd if b == 1 else odd
                keep = jnp.where(
                    lane < TILE, window[tile, side, 2 * g], window[tile, side, 2 * g + 1]
                )
                s = jnp.where(keep > 0, s, -jnp.inf)
            parts.append(s)
        top = jnp.maximum(jnp.maximum(parts[0], parts[1]), parts[2])
        top = jnp.max(top, axis=0, keepdims=True)
        weights = [jnp.exp(s - top) for s in parts]
        total = jnp.sum(weights[0] + weights[1] + weights[2], axis=0, keepdims=True)
        scale = 1.0 / total
        for b, w in enumerate(weights):
            pt_ref[g, pl.ds(b * TILE, TILE), :] = (w * scale).astype(jnp.bfloat16)


def out_kernel(pt, q, v0, v1, v2, after, pon_ref, pof_ref):
    for g in range(pt.shape[0]):
        pon_ref[g, :TILE] = pt[g, TILE : 2 * TILE]
        pof_ref[g, :TILE] = pt[g, 2 * TILE :]
        for n in range(2):
            cols = pl.ds((2 * g + n) * HEAD_DIM, HEAD_DIM)
            lanes = pl.ds(n * HEAD_DIM, HEAD_DIM)
            values = jnp.concatenate([v0[:, cols], v1[:, cols], v2[:, cols]], axis=0)
            out = dot_nn(pt[g, :, lanes].T, values).astype(jnp.bfloat16)
            pon_ref[g, pl.ds(TILE, TILE), lanes] = out
            pof_ref[g, pl.ds(TILE, TILE), lanes] = out
        queries = q[:, pair_cols(g)]
        pon_ref[g, 2 * TILE :] = queries
        pof_ref[g, 2 * TILE :] = queries


def turn_kernel(po, qbd):
    qbd[...] = jnp.zeros_like(qbd)
    for g in range(qbd.shape[0]):
        put_diagonal(qbd, g, po[g, 2 * TILE :])


def mark_kernel(*refs):
    refs[-1][...] = jnp.zeros_like(refs[-1])


def begin_kernel(xa_ref, wot, acc_ref, copy_ref):
    x = xa_ref[...]
    copy_ref[...] = x
    acc_ref[...] = dot_nn(x, wot[: x.shape[1], :])


def fill_diagonal(bd, wot, x, acc_ref):
    bd[...] = jnp.zeros_like(bd)
    start = wot.shape[0] - x.shape[1]
    for g in range(bd.shape[0]):
        cols = pair_cols(g)
        d_out = dot_nn(x, wot[start:, cols])
        if acc_ref is not None:
            d_out = acc_ref[:, cols] + d_out
        put_diagonal(bd, g, d_out.astype(jnp.bfloat16))


def own_attention(scaling, bd, pt, v0, v1, v2, dp, ds_ref):
    for g in range(pt.shape[0]):
        cols = pair_cols(g)
        values = jnp.concatenate([v0[:, cols], v1[:, cols], v2[:, cols]], axis=0)
        dp[g] = dot_nt(values, bd[g])
    for g in range(pt.shape[0]):
        pf = pt[g].astype(jnp.float32)
        delta = jnp.sum(pf * dp[g], axis=0, keepdims=True)
        ds_ref[g] = (pf * ((dp[g] - delta) * scaling)).astype(jnp.bfloat16)


def put_dq(ds, kt, turned, dq):
    for h in range(kt.shape[0]):
        turned[h] = dot_nn(kt[h], ds[h // 2, :, pl.ds((h % 2) * TILE, TILE)])
    for h in range(kt.shape[0]):
        dq[:, pl.ds(h * HEAD_DIM, HEAD_DIM)] = turned[h].T.astype(jnp.bfloat16)


def project_pair(dk, dv, wkt, wvt, part):
    return dot_nn(dk[...], wkt[:, part]) + dot_nn(dv[...], wvt[:, part])


def first_far_kernel(
    scaling, x, wot, qbd, pt, v0, v1, v2, wkt, wvt, after, far_ref, ds_ref, bd, dk, dv, dp
):
    fill_diagonal(bd, wot, x[...], None)
    own_attention(scaling, bd, pt, v0, v1, v2, dp, ds_ref)
    for g in range(pt.shape[0]):
        cols = pair_cols(g)
        dv[:, cols] = dot_nn(pt[g, 2 * TILE :], bd[g]).astype(jnp.bfloat16)
        dk[:, cols] = dot_nn(ds_ref[g, 2 * TILE :], qbd[g]).astype(jnp.bfloat16)
    far_ref[...] = project_pair(dk, dv, wkt, wvt, slice(None)).astype(jnp.bfloat16)


def first_near_kernel(ds_ref, bd, qbd, pt, wkt, wvt, near_ref, dk, dv):
    for g in range(pt.shape[0]):
        cols = pair_cols(g)
        dv[:, cols] = dot_nn(pt[g, TILE : 2 * TILE], bd[g]).astype(jnp.bfloat16)
        dk[:, cols] = dot_nn(ds_ref[g, TILE : 2 * TILE], qbd[g]).astype(jnp.bfloat16)
    near_ref[...] = project_pair(dk, dv, wkt, wvt, slice(None)).astype(jnp.bfloat16)


def first_own_kernel(
    x, ds_ref, bd, qbd, pt, kt, wqt, wkt, wvt, after, base_ref, dq, dk, dv, turned
):
    for g in range(pt.shape[0]):
        cols = pair_cols(g)
        dv[:, cols] = dot_nn(pt[g, :TILE], bd[g]).astype(jnp.bfloat16)
        dk[:, cols] = dot_nn(ds_ref[g, :TILE], qbd[g]).astype(jnp.bfloat16)
    put_dq(ds_ref, kt, turned, dq)
    base = project_pair(dk, dv, wkt, wvt, slice(None)) + dot_nn(dq[...], wqt[...])
    base_ref[...] = base + x[...].astype(jnp.float32)


def first_sum_kernel(base, near, far, after, suma_ref, sumb_ref):
    total = base[...] + near[...].astype(jnp.float32) + far[...].astype(jnp.float32)
    total = total.astype(jnp.bfloat16)
    split = suma_ref.shape[1]
    suma_ref[...] = total[:, :split]
    sumb_ref[...] = total[:, split:]


def halo_attention(scaling, bd, po, v, both, ds_ref):
    for g in range(po.shape[0]):
        values = jnp.concatenate([v[:, pair_cols(g)], po[g, TILE : 2 * TILE]], axis=0)
        both[g] = dot_nt(values, bd[g])
    row = lax.broadcasted_iota(jnp.int32, (TILE, 2 * TILE), 0)
    col = lax.broadcasted_iota(jnp.int32, (TILE, 2 * TILE), 1)
    same = (row == col) | (row + TILE == col)
    for g in range(po.shape[0]):
        delta = jnp.sum(jnp.where(same, both[g, TILE:], 0.0), axis=0, keepdims=True)
        ds = po[g, :TILE].astype(jnp.float32) * ((both[g, :TILE] - delta) * scaling)
        ds_ref[g] = ds.astype(jnp.bfloat16)


def own_kernel(
    scaling,
    acc,
    xb,
    wot,
    qbd,
    pt,
    kt,
    v0,
    v1,
    v2,
    dq,
    dk_ref,
    dv_ref,
    bd,
    dp,
    ds,
    turned,
):
    fill_diagonal(bd, wot, xb[...], acc)
    own_attention(scaling, bd, pt, v0, v1, v2, dp, ds)
    for g in range(pt.shape[0]):
        cols = pair_cols(g)
        dv_ref[:, cols] = dot_nn(pt[g, :TILE], bd[g])
        dk_ref[:, cols] = dot_nn(ds[g, :TILE], qbd[g])
    put_dq(ds, kt, turned, dq)


def near_kernel(
    scaling, xfa, xa, xb, wot, qbd, po, v, dk_in, dv_in, acc_ref, dk_ref, dv_ref, bd, both, ds
):
    x = jnp.concatenate([xa[...], xb[...]], axis=1)
    fill_diagonal(bd, wot, x, None)
    halo_attention(scaling, bd, po, v, both, ds)
    for g in range(po.shape[0]):
        cols = pair_cols(g)
        dv_ref[:, cols] = dv_in[:, cols] + dot_nn(po[g, :TILE], bd[g])
        dk_ref[:, cols] = dk_in[:, cols] + dot_nn(ds[g], qbd[g])
    acc_ref[...] = dot_nn(xfa[...], wot[: xfa.shape[1], :])


def far_kernel(
    scaling,
    acc,
    xb,
    wot,
    qbd,
    po,
    v,
    dk_in,
    dv_in,
    dq,
    own_x,
    wqt,
    wkt,
    wvt,
    sum_ref,
    dk_ref,
    dv_ref,
    bd,
    both,
    ds,
):
    fill_diagonal(bd, wot, xb[...], acc)
    halo_attention(scaling, bd, po, v, both, ds)
    for g in range(po.shape[0]):
        cols = pair_cols(g)
        dv = dv_in[:, cols] + dot_nn(po[g, :TILE], bd[g])
        dk = dk_in[:, cols] + dot_nn(ds[g], qbd[g])
        dv_ref[:, cols] = dv.astype(jnp.bfloat16)
        dk_ref[:, cols] = dk.astype(jnp.bfloat16)
    part = pl.ds(0, sum_ref.shape[1])
    total = own_x[...].astype(jnp.float32) + dot_nn(dq[...], wqt[:, part])
    total = total + project_pair(dk_ref, dv_ref, wkt, wvt, part)
    sum_ref[...] = total.astype(jnp.bfloat16)


def rest_kernel(dk, dv, dq, own_x, wqt, wkt, wvt, sum_ref):
    rest = sum_ref.shape[1]
    part = pl.ds(wqt.shape[1] - rest, rest)
    total = own_x[...].astype(jnp.float32) + dot_nn(dq[...], wqt[:, part])
    total = total + project_pair(dk, dv, wkt, wvt, part)
    sum_ref[...] = total.astype(jnp.bfloat16)


def pick_kernel(*refs):
    done_refs, out_ref = refs[:-1], refs[-1]
    position = lax.axis_index("pipe")
    count = len(done_refs) // 2
    split = done_refs[0].shape[1]
    for step in range(count):

        @pl.when(position == count - 1 - step)
        def _():
            out_ref[:, :split] = done_refs[2 * step][...]
            out_ref[:, split:] = done_refs[2 * step + 1][...]


def body(
    query_rows,
    key_rows,
    value_rows,
    query_weight,
    key_weight,
    value_weight,
    out_weight,
    upstream,
    window,
):
    sections = lax.axis_size("pipe")
    seq_size = lax.axis_size("seq")
    rows, width = query_rows.shape[1:]
    model = out_weight.shape[2]
    split = model // 2
    heads = width // HEAD_DIM
    pairs = heads // 2
    scaling = HEAD_DIM ** (-0.5)
    near_pairs = [(i, i ^ 1) for i in range(seq_size)]
    far_pairs = [(i, i + 1) for i in range(1, seq_size - 1, 2)]
    far_pairs = far_pairs + [(j, i) for i, j in far_pairs]

    def near(value):
        return lax.ppermute(value, "seq", near_pairs)

    def far(value):
        return lax.ppermute(value, "seq", far_pairs)

    def hop(value, source):
        return lax.ppermute(value, "pipe", [(source, source - 1)])

    vmem = pl.BlockSpec(memory_space=pltpu.VMEM)
    smem = pl.BlockSpec(memory_space=pltpu.SMEM)
    anywhere = pl.BlockSpec(memory_space=pl.ANY)
    bf16, f32 = jnp.bfloat16, jnp.float32
    weight = pltpu.VMEM((model, width), bf16)
    block = (pairs, 2 * TILE, 2 * HEAD_DIM)
    tile = pltpu.VMEM((rows, width), bf16)
    wide = pltpu.VMEM((rows, width), f32)
    whole = jax.ShapeDtypeStruct((rows, model), bf16)
    piece_a = jax.ShapeDtypeStruct((rows, split), bf16)
    piece_b = jax.ShapeDtypeStruct((rows, model - split), bf16)
    dp_scratch = pltpu.VMEM((pairs, 3 * TILE, 2 * TILE), f32)
    turned_scratch = pltpu.VMEM((heads, HEAD_DIM, TILE), f32)
    halo_scratch = [
        pltpu.VMEM(block, bf16),
        pltpu.VMEM(block, f32),
        pltpu.VMEM((pairs, TILE, 2 * TILE), bf16),
    ]
    diagonal = pltpu.VMEM(block, bf16)

    def call(kernel, name, ins, outs, scratch=(), limit=12, cost=0):
        single = not isinstance(outs, list)
        estimate = pl.CostEstimate(flops=cost, bytes_accessed=0, transcendentals=0)
        return pl.pallas_call(
            kernel,
            in_specs=ins,
            out_specs=vmem if single else [vmem] * len(outs),
            out_shape=outs,
            scratch_shapes=list(scratch),
            compiler_params=pltpu.CompilerParams(vmem_limit_bytes=limit * MIB),
            cost_estimate=estimate if cost else None,
            name=name,
        )

    def mark(*values):
        token = pltpu.VMEM((8, 128), f32)
        return call(mark_kernel, "mark", [anywhere] * len(values), token, cost=10**10)(*values)

    k2 = far(key_rows[0])
    v2 = far(value_rows[0])
    wot, wkt, wvt, wqt, q, k, v, x, qbd = call(
        prep_kernel,
        "prep",
        [anywhere] * 8,
        [weight, weight, weight, weight, tile, tile, tile, tile, diagonal],
        [pltpu.VMEM((4, model, width), bf16), pltpu.SemaphoreType.DMA((20,))],
        36,
    )(
        out_weight[0],
        key_weight[0],
        value_weight[0],
        query_weight[0],
        query_rows[0],
        key_rows[0],
        value_rows[0],
        upstream,
    )
    k1 = near(k)
    v1 = near(v)
    pt, kt = call(
        functools.partial(prob_kernel, scaling),
        "prob",
        [smem] + [vmem] * 4 + [anywhere],
        [
            pltpu.VMEM((pairs, 3 * TILE, 2 * rows), bf16),
            pltpu.VMEM((heads, HEAD_DIM, 3 * TILE), bf16),
        ],
        [dp_scratch],
    )(jnp.transpose(window, (0, 2, 1)), qbd, k, k1, k2, mark(k2))

    to_far, ds, bd = call(
        functools.partial(first_far_kernel, scaling),
        "first_far",
        [vmem] * 9 + [anywhere],
        [whole, pltpu.VMEM((pairs, 3 * TILE, 2 * rows), bf16), diagonal],
        [tile, tile, dp_scratch],
    )(x, wot, qbd, pt, v, v1, v2, wkt, wvt, mark(v2, pt))
    from_far = far(to_far)
    to_near = call(first_near_kernel, "first_near", [vmem] * 6, whole, [tile, tile])(
        ds, bd, qbd, pt, wkt, wvt
    )
    from_near = near(to_near)
    packet = pltpu.VMEM((pairs, 3 * TILE, 2 * HEAD_DIM), bf16)
    po_to_near, po_to_far = call(out_kernel, "out", [vmem] * 5 + [anywhere], [packet, packet])(
        pt, q, v, v1, v2, to_near
    )
    pof = far(po_to_far)
    pon = near(po_to_near)
    turn = call(turn_kernel, "turn", [vmem], diagonal)
    qbdn, qbdf = turn(pon), turn(pof)
    base = call(
        first_own_kernel,
        "first_own",
        [vmem] * 9 + [anywhere],
        wide,
        [tile, tile, tile, turned_scratch],
    )(x, ds, bd, qbd, pt, kt, wqt, wkt, wvt, po_to_far)
    done_a, done_b = call(
        first_sum_kernel, "first_sum", [vmem] * 3 + [anywhere], [piece_a, piece_b]
    )(base, from_near, from_far, mark(from_far))
    done = [done_a, done_b]

    for step in range(1, sections):
        source = sections - step
        xa = hop(done_a, source)
        xb = hop(done_b, source)
        acc, xa_copy = call(begin_kernel, "begin", [vmem] * 2, [wide, piece_a])(xa, wot)
        xfa, xfb = far(xa_copy), far(xb)
        xna, xnb = near(xa_copy), near(xb)
        dq, dk, dv = call(
            functools.partial(own_kernel, scaling),
            "own",
            [vmem] * 9,
            [tile, wide, wide],
            [
                pltpu.VMEM(block, bf16),
                dp_scratch,
                pltpu.VMEM((pairs, 3 * TILE, 2 * TILE), bf16),
                turned_scratch,
            ],
        )(acc, xb, wot, qbd, pt, kt, v, v1, v2)
        acc, dk, dv = call(
            functools.partial(near_kernel, scaling),
            "near",
            [vmem] * 9,
            [wide, wide, wide],
            halo_scratch,
        )(xfa, xna, xnb, wot, qbdn, pon, v, dk, dv)
        done_a, dk, dv = call(
            functools.partial(far_kernel, scaling),
            "far",
            [vmem] * 13,
            [piece_a, tile, tile],
            halo_scratch,
        )(acc, xfb, wot, qbdf, pof, v, dk, dv, dq, xa, wqt, wkt, wvt)
        done_b = call(rest_kernel, "rest", [vmem] * 7, piece_b)(dk, dv, dq, xb, wqt, wkt, wvt)
        done += [done_a, done_b]
    out = call(pick_kernel, "pick", [vmem] * (2 * sections), jax.ShapeDtypeStruct((rows, model), bf16))
    return out(*done)[None]


def solution(mesh):
    in_specs = (
        P("pipe", "seq", None),
        P("pipe", "seq", None),
        P("pipe", "seq", None),
        P("pipe", None, None),
        P("pipe", None, None),
        P("pipe", None, None),
        P("pipe", None, None),
        P("seq", None),
        P(),
    )
    out_specs = P("pipe", "seq", None)
    return jax.shard_map(body, mesh=mesh, in_specs=in_specs, out_specs=out_specs, check_vma=False)
```

```python
import functools

import jax
import jax.numpy as jnp
from jax import lax
from jax.experimental import pallas as pl
from jax.experimental.pallas import tpu as pltpu
from jax.sharding import PartitionSpec as P

HEAD_DIM = 128
TILE = 128
MIB = 1 << 20


def dot_nt(a, b):
    return lax.dot_general(a, b, (((1,), (1,)), ((), ())), preferred_element_type=jnp.float32)


def dot_nn(a, b):
    return lax.dot_general(a, b, (((1,), (0,)), ((), ())), preferred_element_type=jnp.float32)


def pair_cols(g):
    return pl.ds(g * 2 * HEAD_DIM, 2 * HEAD_DIM)


def put_diagonal(target, g, value):
    target[g, pl.ds(0, TILE), pl.ds(0, HEAD_DIM)] = value[:, :HEAD_DIM]
    target[g, pl.ds(TILE, TILE), pl.ds(HEAD_DIM, HEAD_DIM)] = value[:, HEAD_DIM:]


def prep_kernel(
    wo_hbm,
    wk_hbm,
    wv_hbm,
    wq_hbm,
    q_hbm,
    k_hbm,
    v_hbm,
    x_hbm,
    wot,
    wkt,
    wvt,
    wqt,
    q,
    k,
    v,
    x,
    qbd,
    raw,
    sems,
):
    groups = 4
    rows = raw.shape[1] // groups
    small = [
        pltpu.make_async_copy(src, dst, sems.at[n])
        for n, (src, dst) in enumerate(((q_hbm, q), (k_hbm, k), (v_hbm, v), (x_hbm, x)))
    ]
    large = []
    for n, src in enumerate((wo_hbm, wk_hbm, wv_hbm, wq_hbm)):
        for g in range(groups):
            part = pl.ds(g * rows, rows)
            sem = sems.at[4 + n * groups + g]
            large.append(pltpu.make_async_copy(src.at[part], raw.at[n, part], sem))
    for copy in small + large:
        copy.start()
    qbd[...] = jnp.zeros_like(qbd)
    for copy in small:
        copy.wait()
    for g in range(qbd.shape[0]):
        put_diagonal(qbd, g, q[:, pair_cols(g)])
    for n, dst in enumerate((wot, wkt, wvt, wqt)):
        for g in range(groups):
            large[n * groups + g].wait()

            @pl.loop(0, rows // TILE)
            def _(r, n=n, g=g, dst=dst):
                part = pl.ds(pl.multiple_of(g * rows + r * TILE, TILE), TILE)
                dst[:, part] = raw[n, part, :].T


def prob_kernel(scaling, window, qbd, k0, k1, k2, after, pt_ref, kt_ref, scores):
    pairs = pt_ref.shape[0]
    tile = lax.axis_index("seq")
    odd = lax.rem(tile, 2)
    for g in range(pairs):
        cols = pair_cols(g)
        keys = jnp.concatenate([k0[:, cols], k1[:, cols], k2[:, cols]], axis=0)
        scores[g] = dot_nt(keys, qbd[g])
        for b, k_ref in enumerate((k0, k1, k2)):
            for n in range(2):
                h = 2 * g + n
                part = k_ref[:, pl.ds(h * HEAD_DIM, HEAD_DIM)]
                kt_ref[h, :, pl.ds(b * TILE, TILE)] = part.T
    lane = lax.broadcasted_iota(jnp.int32, (TILE, 2 * TILE), 1)
    for g in range(pairs):
        parts = []
        for b in range(3):
            s = scaling * scores[g, pl.ds(b * TILE, TILE)]
            if b > 0:
                side = 1 - odd if b == 1 else odd
                keep = jnp.where(
                    lane < TILE, window[tile, side, 2 * g], window[tile, side, 2 * g + 1]
                )
                s = jnp.where(keep > 0, s, -jnp.inf)
            parts.append(s)
        top = jnp.maximum(jnp.maximum(parts[0], parts[1]), parts[2])
        top = jnp.max(top, axis=0, keepdims=True)
        weights = [jnp.exp(s - top) for s in parts]
        total = jnp.sum(weights[0] + weights[1] + weights[2], axis=0, keepdims=True)
        scale = 1.0 / total
        for b, w in enumerate(weights):
            pt_ref[g, pl.ds(b * TILE, TILE), :] = (w * scale).astype(jnp.bfloat16)


def out_kernel(pt, q, v0, v1, v2, after, pon_ref, pof_ref):
    for g in range(pt.shape[0]):
        pon_ref[g, :TILE] = pt[g, TILE : 2 * TILE]
        pof_ref[g, :TILE] = pt[g, 2 * TILE :]
        for n in range(2):
            cols = pl.ds((2 * g + n) * HEAD_DIM, HEAD_DIM)
            lanes = pl.ds(n * HEAD_DIM, HEAD_DIM)
            values = jnp.concatenate([v0[:, cols], v1[:, cols], v2[:, cols]], axis=0)
            out = dot_nn(pt[g, :, lanes].T, values).astype(jnp.bfloat16)
            pon_ref[g, pl.ds(TILE, TILE), lanes] = out
            pof_ref[g, pl.ds(TILE, TILE), lanes] = out
        queries = q[:, pair_cols(g)]
        pon_ref[g, 2 * TILE :] = queries
        pof_ref[g, 2 * TILE :] = queries


def turn_kernel(po, qbd):
    qbd[...] = jnp.zeros_like(qbd)
    for g in range(qbd.shape[0]):
        put_diagonal(qbd, g, po[g, 2 * TILE :])


def mark_kernel(*refs):
    refs[-1][...] = jnp.zeros_like(refs[-1])


def begin_kernel(xa_ref, wot, acc_ref, copy_ref):
    x = xa_ref[...]
    copy_ref[...] = x
    acc_ref[...] = dot_nn(x, wot[: x.shape[1], :])


def fill_diagonal(bd, wot, x, acc_ref):
    bd[...] = jnp.zeros_like(bd)
    start = wot.shape[0] - x.shape[1]
    for g in range(bd.shape[0]):
        cols = pair_cols(g)
        d_out = dot_nn(x, wot[start:, cols])
        if acc_ref is not None:
            d_out = acc_ref[:, cols] + d_out
        put_diagonal(bd, g, d_out.astype(jnp.bfloat16))


def own_attention(scaling, bd, pt, v0, v1, v2, dp, ds_ref):
    for g in range(pt.shape[0]):
        cols = pair_cols(g)
        values = jnp.concatenate([v0[:, cols], v1[:, cols], v2[:, cols]], axis=0)
        dp[g] = dot_nt(values, bd[g])
    for g in range(pt.shape[0]):
        pf = pt[g].astype(jnp.float32)
        delta = jnp.sum(pf * dp[g], axis=0, keepdims=True)
        ds_ref[g] = (pf * ((dp[g] - delta) * scaling)).astype(jnp.bfloat16)


def put_dq(ds, kt, turned, dq):
    for h in range(kt.shape[0]):
        turned[h] = dot_nn(kt[h], ds[h // 2, :, pl.ds((h % 2) * TILE, TILE)])
    for h in range(kt.shape[0]):
        dq[:, pl.ds(h * HEAD_DIM, HEAD_DIM)] = turned[h].T.astype(jnp.bfloat16)


def project_pair(dk, dv, wkt, wvt, part):
    return dot_nn(dk[...], wkt[:, part]) + dot_nn(dv[...], wvt[:, part])


def first_far_kernel(
    scaling, x, wot, qbd, pt, v0, v1, v2, wkt, wvt, after, far_ref, ds_ref, bd, dk, dv, dp
):
    fill_diagonal(bd, wot, x[...], None)
    own_attention(scaling, bd, pt, v0, v1, v2, dp, ds_ref)
    for g in range(pt.shape[0]):
        cols = pair_cols(g)
        dv[:, cols] = dot_nn(pt[g, 2 * TILE :], bd[g]).astype(jnp.bfloat16)
        dk[:, cols] = dot_nn(ds_ref[g, 2 * TILE :], qbd[g]).astype(jnp.bfloat16)
    far_ref[...] = project_pair(dk, dv, wkt, wvt, slice(None)).astype(jnp.bfloat16)


def first_near_kernel(ds_ref, bd, qbd, pt, wkt, wvt, near_ref, dk, dv):
    for g in range(pt.shape[0]):
        cols = pair_cols(g)
        dv[:, cols] = dot_nn(pt[g, TILE : 2 * TILE], bd[g]).astype(jnp.bfloat16)
        dk[:, cols] = dot_nn(ds_ref[g, TILE : 2 * TILE], qbd[g]).astype(jnp.bfloat16)
    near_ref[...] = project_pair(dk, dv, wkt, wvt, slice(None)).astype(jnp.bfloat16)


def first_own_kernel(
    x, ds_ref, bd, qbd, pt, kt, wqt, wkt, wvt, after, base_ref, dq, dk, dv, turned
):
    for g in range(pt.shape[0]):
        cols = pair_cols(g)
        dv[:, cols] = dot_nn(pt[g, :TILE], bd[g]).astype(jnp.bfloat16)
        dk[:, cols] = dot_nn(ds_ref[g, :TILE], qbd[g]).astype(jnp.bfloat16)
    put_dq(ds_ref, kt, turned, dq)
    base = project_pair(dk, dv, wkt, wvt, slice(None)) + dot_nn(dq[...], wqt[...])
    base_ref[...] = base + x[...].astype(jnp.float32)


def first_sum_kernel(base, near, far, after, suma_ref, sumb_ref):
    total = base[...] + near[...].astype(jnp.float32) + far[...].astype(jnp.float32)
    total = total.astype(jnp.bfloat16)
    split = suma_ref.shape[1]
    suma_ref[...] = total[:, :split]
    sumb_ref[...] = total[:, split:]


def halo_attention(scaling, bd, po, v, both, ds_ref):
    for g in range(po.shape[0]):
        values = jnp.concatenate([v[:, pair_cols(g)], po[g, TILE : 2 * TILE]], axis=0)
        both[g] = dot_nt(values, bd[g])
    row = lax.broadcasted_iota(jnp.int32, (TILE, 2 * TILE), 0)
    col = lax.broadcasted_iota(jnp.int32, (TILE, 2 * TILE), 1)
    same = (row == col) | (row + TILE == col)
    for g in range(po.shape[0]):
        delta = jnp.sum(jnp.where(same, both[g, TILE:], 0.0), axis=0, keepdims=True)
        ds = po[g, :TILE].astype(jnp.float32) * ((both[g, :TILE] - delta) * scaling)
        ds_ref[g] = ds.astype(jnp.bfloat16)


def own_kernel(
    scaling,
    acc,
    xb,
    wot,
    qbd,
    pt,
    kt,
    v0,
    v1,
    v2,
    dq,
    dk_ref,
    dv_ref,
    bd,
    dp,
    ds,
    turned,
):
    fill_diagonal(bd, wot, xb[...], acc)
    own_attention(scaling, bd, pt, v0, v1, v2, dp, ds)
    for g in range(pt.shape[0]):
        cols = pair_cols(g)
        dv_ref[:, cols] = dot_nn(pt[g, :TILE], bd[g])
        dk_ref[:, cols] = dot_nn(ds[g, :TILE], qbd[g])
    put_dq(ds, kt, turned, dq)


def near_kernel(
    scaling, xfa, xa, xb, wot, qbd, po, v, dk_in, dv_in, acc_ref, dk_ref, dv_ref, bd, both, ds
):
    x = jnp.concatenate([xa[...], xb[...]], axis=1)
    fill_diagonal(bd, wot, x, None)
    halo_attention(scaling, bd, po, v, both, ds)
    for g in range(po.shape[0]):
        cols = pair_cols(g)
        dv_ref[:, cols] = dv_in[:, cols] + dot_nn(po[g, :TILE], bd[g])
        dk_ref[:, cols] = dk_in[:, cols] + dot_nn(ds[g], qbd[g])
    acc_ref[...] = dot_nn(xfa[...], wot[: xfa.shape[1], :])


def far_kernel(
    scaling,
    acc,
    xb,
    wot,
    qbd,
    po,
    v,
    dk_in,
    dv_in,
    dq,
    own_x,
    wqt,
    wkt,
    wvt,
    sum_ref,
    dk_ref,
    dv_ref,
    bd,
    both,
    ds,
):
    fill_diagonal(bd, wot, xb[...], acc)
    halo_attention(scaling, bd, po, v, both, ds)
    for g in range(po.shape[0]):
        cols = pair_cols(g)
        dv = dv_in[:, cols] + dot_nn(po[g, :TILE], bd[g])
        dk = dk_in[:, cols] + dot_nn(ds[g], qbd[g])
        dv_ref[:, cols] = dv.astype(jnp.bfloat16)
        dk_ref[:, cols] = dk.astype(jnp.bfloat16)
    part = pl.ds(0, sum_ref.shape[1])
    total = own_x[...].astype(jnp.float32) + dot_nn(dq[...], wqt[:, part])
    total = total + project_pair(dk_ref, dv_ref, wkt, wvt, part)
    sum_ref[...] = total.astype(jnp.bfloat16)


def rest_kernel(dk, dv, dq, own_x, wqt, wkt, wvt, sum_ref):
    rest = sum_ref.shape[1]
    part = pl.ds(wqt.shape[1] - rest, rest)
    total = own_x[...].astype(jnp.float32) + dot_nn(dq[...], wqt[:, part])
    total = total + project_pair(dk, dv, wkt, wvt, part)
    sum_ref[...] = total.astype(jnp.bfloat16)


def pick_kernel(*refs):
    done_refs, out_ref = refs[:-1], refs[-1]
    position = lax.axis_index("pipe")
    count = len(done_refs) // 2
    split = done_refs[0].shape[1]
    for step in range(count):

        @pl.when(position == count - 1 - step)
        def _():
            out_ref[:, :split] = done_refs[2 * step][...]
            out_ref[:, split:] = done_refs[2 * step + 1][...]


def body(
    query_rows,
    key_rows,
    value_rows,
    query_weight,
    key_weight,
    value_weight,
    out_weight,
    upstream,
    window,
):
    sections = lax.axis_size("pipe")
    seq_size = lax.axis_size("seq")
    rows, width = query_rows.shape[1:]
    model = out_weight.shape[2]
    split = model // 2
    heads = width // HEAD_DIM
    pairs = heads // 2
    scaling = HEAD_DIM ** (-0.5)
    near_pairs = [(i, i ^ 1) for i in range(seq_size)]
    far_pairs = [(i, i + 1) for i in range(1, seq_size - 1, 2)]
    far_pairs = far_pairs + [(j, i) for i, j in far_pairs]

    def near(value):
        return lax.ppermute(value, "seq", near_pairs)

    def far(value):
        return lax.ppermute(value, "seq", far_pairs)

    def hop(value, source):
        return lax.ppermute(value, "pipe", [(source, source - 1)])

    vmem = pl.BlockSpec(memory_space=pltpu.VMEM)
    smem = pl.BlockSpec(memory_space=pltpu.SMEM)
    anywhere = pl.BlockSpec(memory_space=pl.ANY)
    bf16, f32 = jnp.bfloat16, jnp.float32
    weight = pltpu.VMEM((model, width), bf16)
    block = (pairs, 2 * TILE, 2 * HEAD_DIM)
    tile = pltpu.VMEM((rows, width), bf16)
    wide = pltpu.VMEM((rows, width), f32)
    whole = jax.ShapeDtypeStruct((rows, model), bf16)
    piece_a = jax.ShapeDtypeStruct((rows, split), bf16)
    piece_b = jax.ShapeDtypeStruct((rows, model - split), bf16)
    dp_scratch = pltpu.VMEM((pairs, 3 * TILE, 2 * TILE), f32)
    turned_scratch = pltpu.VMEM((heads, HEAD_DIM, TILE), f32)
    halo_scratch = [
        pltpu.VMEM(block, bf16),
        pltpu.VMEM(block, f32),
        pltpu.VMEM((pairs, TILE, 2 * TILE), bf16),
    ]
    diagonal = pltpu.VMEM(block, bf16)

    def call(kernel, name, ins, outs, scratch=(), limit=12, cost=0):
        single = not isinstance(outs, list)
        estimate = pl.CostEstimate(flops=cost, bytes_accessed=0, transcendentals=0)
        return pl.pallas_call(
            kernel,
            in_specs=ins,
            out_specs=vmem if single else [vmem] * len(outs),
            out_shape=outs,
            scratch_shapes=list(scratch),
            compiler_params=pltpu.CompilerParams(vmem_limit_bytes=limit * MIB),
            cost_estimate=estimate if cost else None,
            name=name,
        )

    def mark(*values):
        token = pltpu.VMEM((8, 128), f32)
        return call(mark_kernel, "mark", [anywhere] * len(values), token, cost=10**10)(*values)

    k2 = far(key_rows[0])
    v2 = far(value_rows[0])
    wot, wkt, wvt, wqt, q, k, v, x, qbd = call(
        prep_kernel,
        "prep",
        [anywhere] * 8,
        [weight, weight, weight, weight, tile, tile, tile, tile, diagonal],
        [pltpu.VMEM((4, model, width), bf16), pltpu.SemaphoreType.DMA((20,))],
        36,
    )(
        out_weight[0],
        key_weight[0],
        value_weight[0],
        query_weight[0],
        query_rows[0],
        key_rows[0],
        value_rows[0],
        upstream,
    )
    k1 = near(k)
    v1 = near(v)
    pt, kt = call(
        functools.partial(prob_kernel, scaling),
        "prob",
        [smem] + [vmem] * 4 + [anywhere],
        [
            pltpu.VMEM((pairs, 3 * TILE, 2 * rows), bf16),
            pltpu.VMEM((heads, HEAD_DIM, 3 * TILE), bf16),
        ],
        [dp_scratch],
    )(jnp.transpose(window, (0, 2, 1)), qbd, k, k1, k2, mark(k2))

    to_far, ds, bd = call(
        functools.partial(first_far_kernel, scaling),
        "first_far",
        [vmem] * 9 + [anywhere],
        [whole, pltpu.VMEM((pairs, 3 * TILE, 2 * rows), bf16), diagonal],
        [tile, tile, dp_scratch],
    )(x, wot, qbd, pt, v, v1, v2, wkt, wvt, mark(v2, pt))
    from_far = far(to_far)
    to_near = call(first_near_kernel, "first_near", [vmem] * 6, whole, [tile, tile])(
        ds, bd, qbd, pt, wkt, wvt
    )
    from_near = near(to_near)
    packet = pltpu.VMEM((pairs, 3 * TILE, 2 * HEAD_DIM), bf16)
    po_to_near, po_to_far = call(out_kernel, "out", [vmem] * 5 + [anywhere], [packet, packet])(
        pt, q, v, v1, v2, to_near
    )
    pof = far(po_to_far)
    pon = near(po_to_near)
    turn = call(turn_kernel, "turn", [vmem], diagonal)
    qbdn, qbdf = turn(pon), turn(pof)
    base = call(
        first_own_kernel,
        "first_own",
        [vmem] * 9 + [anywhere],
        wide,
        [tile, tile, tile, turned_scratch],
    )(x, ds, bd, qbd, pt, kt, wqt, wkt, wvt, po_to_far)
    done_a, done_b = call(
        first_sum_kernel, "first_sum", [vmem] * 3 + [anywhere], [piece_a, piece_b]
    )(base, from_near, from_far, mark(from_far))
    done = [done_a, done_b]

    for step in range(1, sections):
        source = sections - step
        xa = hop(done_a, source)
        xb = hop(done_b, source)
        acc, xa_copy = call(begin_kernel, "begin", [vmem] * 2, [wide, piece_a])(xa, wot)
        xfa, xfb = far(xa_copy), far(xb)
        xna, xnb = near(xa_copy), near(xb)
        dq, dk, dv = call(
            functools.partial(own_kernel, scaling),
            "own",
            [vmem] * 9,
            [tile, wide, wide],
            [
                pltpu.VMEM(block, bf16),
                dp_scratch,
                pltpu.VMEM((pairs, 3 * TILE, 2 * TILE), bf16),
                turned_scratch,
            ],
        )(acc, xb, wot, qbd, pt, kt, v, v1, v2)
        acc, dk, dv = call(
            functools.partial(near_kernel, scaling),
            "near",
            [vmem] * 9,
            [wide, wide, wide],
            halo_scratch,
        )(xfa, xna, xnb, wot, qbdn, pon, v, dk, dv)
        done_a, dk, dv = call(
            functools.partial(far_kernel, scaling),
            "far",
            [vmem] * 13,
            [piece_a, tile, tile],
            halo_scratch,
        )(acc, xfb, wot, qbdf, pof, v, dk, dv, dq, xa, wqt, wkt, wvt)
        done_b = call(rest_kernel, "rest", [vmem] * 7, piece_b)(dk, dv, dq, xb, wqt, wkt, wvt)
        done += [done_a, done_b]
    out = call(pick_kernel, "pick", [vmem] * (2 * sections), jax.ShapeDtypeStruct((rows, model), bf16))
    return out(*done)[None]


def solution(mesh):
    in_specs = (
        P("pipe", "seq", None),
        P("pipe", "seq", None),
        P("pipe", "seq", None),
        P("pipe", None, None),
        P("pipe", None, None),
        P("pipe", None, None),
        P("pipe", None, None),
        P("seq", None),
        P(),
    )
    out_specs = P("pipe", "seq", None)
    return jax.shard_map(body, mesh=mesh, in_specs=in_specs, out_specs=out_specs, check_vma=False)
```

```python
import functools

import jax
import jax.numpy as jnp
from jax import lax
from jax.experimental import pallas as pl
from jax.experimental.pallas import tpu as pltpu
from jax.sharding import PartitionSpec as P

HEAD_DIM = 128
TILE = 128
MIB = 1 << 20


def dot_nt(a, b):
    return lax.dot_general(a, b, (((1,), (1,)), ((), ())), preferred_element_type=jnp.float32)


def dot_nn(a, b):
    return lax.dot_general(a, b, (((1,), (0,)), ((), ())), preferred_element_type=jnp.float32)


def pair_cols(g):
    return pl.ds(g * 2 * HEAD_DIM, 2 * HEAD_DIM)


def put_diagonal(target, g, value):
    target[g, pl.ds(0, TILE), pl.ds(0, HEAD_DIM)] = value[:, :HEAD_DIM]
    target[g, pl.ds(TILE, TILE), pl.ds(HEAD_DIM, HEAD_DIM)] = value[:, HEAD_DIM:]


def prep_kernel(
    wo_hbm,
    wk_hbm,
    wv_hbm,
    wq_hbm,
    q_hbm,
    k_hbm,
    v_hbm,
    x_hbm,
    window,
    wot,
    wkt,
    wvt,
    wqt,
    q,
    k,
    v,
    x,
    qbd,
    keep,
    raw,
    flags,
    sems,
):
    groups = 4
    rows = raw.shape[1] // groups
    small = [
        pltpu.make_async_copy(src, dst, sems.at[n])
        for n, (src, dst) in enumerate(((q_hbm, q), (k_hbm, k), (v_hbm, v), (x_hbm, x)))
    ]
    sources = (wo_hbm, wk_hbm, wv_hbm, wq_hbm)

    def large(n, g):
        part = pl.ds(g * rows, rows)
        return pltpu.make_async_copy(
            sources[n].at[part], raw.at[n, part], sems.at[4 + n * groups + g]
        )

    window_copy = pltpu.make_async_copy(window, flags, sems.at[20])
    window_copy.start()
    for copy in small:
        copy.start()
    for n in range(len(sources)):
        for g in range(groups):
            large(n, g).start()
    qbd[...] = jnp.zeros_like(qbd)
    for copy in small:
        copy.wait()
    for g in range(qbd.shape[0]):
        put_diagonal(qbd, g, q[:, pair_cols(g)])
    for n, dst in enumerate((wot, wkt, wvt, wqt)):

        @pl.loop(0, groups)
        def _(g, n=n, dst=dst):
            start = pl.multiple_of(g * rows, rows)
            large(n, g).wait()
            for r in range(0, rows, TILE):
                part = pl.ds(start + r, TILE)
                dst[:, part] = raw[n, part, :].T
    window_copy.wait()
    tile = lax.axis_index("seq")
    odd = lax.rem(tile, 2)
    lane = lax.broadcasted_iota(jnp.int32, keep.shape[2:], 1)
    for b, side in enumerate((1 - odd, odd)):
        for g in range(keep.shape[1]):
            keep[b, g] = jnp.where(
                lane < TILE, flags[tile, side, 2 * g], flags[tile, side, 2 * g + 1]
            )


def prob_kernel(scaling, keep, qbd, k0, k1, k2, after, pt_ref, kt_ref, scores):
    pairs = pt_ref.shape[0]
    for g in range(pairs):
        cols = pair_cols(g)
        keys = jnp.concatenate([k0[:, cols], k1[:, cols], k2[:, cols]], axis=0)
        scores[g] = dot_nt(keys, qbd[g])
        for b, k_ref in enumerate((k0, k1, k2)):
            for n in range(2):
                h = 2 * g + n
                part = k_ref[:, pl.ds(h * HEAD_DIM, HEAD_DIM)]
                kt_ref[h, :, pl.ds(b * TILE, TILE)] = part.T
    for g in range(pairs):
        parts = []
        for b in range(3):
            s = scaling * scores[g, pl.ds(b * TILE, TILE)]
            if b > 0:
                s = jnp.where(keep[b - 1, g, 0:1] > 0, s, -jnp.inf)
            parts.append(s)
        top = jnp.maximum(jnp.maximum(parts[0], parts[1]), parts[2])
        top = jnp.max(top, axis=0, keepdims=True)
        weights = [jnp.exp(s - top) for s in parts]
        total = jnp.sum(weights[0] + weights[1] + weights[2], axis=0, keepdims=True)
        scale = 1.0 / total
        for b, w in enumerate(weights):
            pt_ref[g, pl.ds(b * TILE, TILE), :] = (w * scale).astype(jnp.bfloat16)


def out_kernel(pt, q, v0, v1, v2, after, pon_ref, pof_ref):
    for g in range(pt.shape[0]):
        pon_ref[g, :TILE] = pt[g, TILE : 2 * TILE]
        pof_ref[g, :TILE] = pt[g, 2 * TILE :]
        for n in range(2):
            cols = pl.ds((2 * g + n) * HEAD_DIM, HEAD_DIM)
            lanes = pl.ds(n * HEAD_DIM, HEAD_DIM)
            values = jnp.concatenate([v0[:, cols], v1[:, cols], v2[:, cols]], axis=0)
            out = dot_nn(pt[g, :, lanes].T, values).astype(jnp.bfloat16)
            pon_ref[g, pl.ds(TILE, TILE), lanes] = out
            pof_ref[g, pl.ds(TILE, TILE), lanes] = out
        queries = q[:, pair_cols(g)]
        pon_ref[g, 2 * TILE :] = queries
        pof_ref[g, 2 * TILE :] = queries


def turn_kernel(po, qbd):
    qbd[...] = jnp.zeros_like(qbd)
    for g in range(qbd.shape[0]):
        put_diagonal(qbd, g, po[g, 2 * TILE :])


def mark_kernel(*refs):
    refs[-1][...] = jnp.zeros_like(refs[-1])


def begin_kernel(xa_ref, wot, after, acc_ref, copy_ref):
    x = xa_ref[...]
    copy_ref[...] = x
    acc_ref[...] = dot_nn(x, wot[: x.shape[1], :])


def fill_diagonal(bd, wot, x, acc_ref):
    bd[...] = jnp.zeros_like(bd)
    start = wot.shape[0] - x.shape[1]
    for g in range(bd.shape[0]):
        cols = pair_cols(g)
        d_out = dot_nn(x, wot[start:, cols])
        if acc_ref is not None:
            d_out = acc_ref[:, cols] + d_out
        put_diagonal(bd, g, d_out.astype(jnp.bfloat16))


def own_attention(scaling, bd, pt, v0, v1, v2, dp, ds_ref):
    for g in range(pt.shape[0]):
        cols = pair_cols(g)
        values = jnp.concatenate([v0[:, cols], v1[:, cols], v2[:, cols]], axis=0)
        dp[g] = dot_nt(values, bd[g])
    for g in range(pt.shape[0]):
        pf = pt[g].astype(jnp.float32)
        delta = jnp.sum(pf * dp[g], axis=0, keepdims=True)
        ds_ref[g] = (pf * ((dp[g] - delta) * scaling)).astype(jnp.bfloat16)


def put_dq(ds, kt, turned, dq):
    for h in range(kt.shape[0]):
        turned[h] = dot_nn(kt[h], ds[h // 2, :, pl.ds((h % 2) * TILE, TILE)])
    for h in range(kt.shape[0]):
        dq[:, pl.ds(h * HEAD_DIM, HEAD_DIM)] = turned[h].T.astype(jnp.bfloat16)


def project_pair(dk, dv, wkt, wvt, part):
    return dot_nn(dk[...], wkt[:, part]) + dot_nn(dv[...], wvt[:, part])


def first_far_kernel(
    last, scaling, x, wot, qbd, pt, v0, v1, v2, wkt, wvt, after, far_ref, ds_ref, bd, dk, dv, dp
):
    @pl.when(lax.axis_index("pipe") == last)
    def _():
        fill_diagonal(bd, wot, x[...], None)
        own_attention(scaling, bd, pt, v0, v1, v2, dp, ds_ref)
        for g in range(pt.shape[0]):
            cols = pair_cols(g)
            dv[:, cols] = dot_nn(pt[g, 2 * TILE :], bd[g]).astype(jnp.bfloat16)
            dk[:, cols] = dot_nn(ds_ref[g, 2 * TILE :], qbd[g]).astype(jnp.bfloat16)
        far_ref[...] = project_pair(dk, dv, wkt, wvt, slice(None)).astype(jnp.bfloat16)


def first_near_kernel(last, ds_ref, bd, qbd, pt, wkt, wvt, near_ref, dk, dv):
    @pl.when(lax.axis_index("pipe") == last)
    def _():
        for g in range(pt.shape[0]):
            cols = pair_cols(g)
            dv[:, cols] = dot_nn(pt[g, TILE : 2 * TILE], bd[g]).astype(jnp.bfloat16)
            dk[:, cols] = dot_nn(ds_ref[g, TILE : 2 * TILE], qbd[g]).astype(jnp.bfloat16)
        near_ref[...] = project_pair(dk, dv, wkt, wvt, slice(None)).astype(jnp.bfloat16)


def first_own_kernel(
    last, x, ds_ref, bd, qbd, pt, kt, wqt, wkt, wvt, after, base_ref, dq, dk, dv, turned
):
    @pl.when(lax.axis_index("pipe") == last)
    def _():
        for g in range(pt.shape[0]):
            cols = pair_cols(g)
            dv[:, cols] = dot_nn(pt[g, :TILE], bd[g]).astype(jnp.bfloat16)
            dk[:, cols] = dot_nn(ds_ref[g, :TILE], qbd[g]).astype(jnp.bfloat16)
        put_dq(ds_ref, kt, turned, dq)
        base = project_pair(dk, dv, wkt, wvt, slice(None)) + dot_nn(dq[...], wqt[...])
        base_ref[...] = base + x[...].astype(jnp.float32)


def first_sum_kernel(base, near, far, after, suma_ref, sumb_ref):
    total = base[...] + near[...].astype(jnp.float32) + far[...].astype(jnp.float32)
    total = total.astype(jnp.bfloat16)
    split = suma_ref.shape[1]
    suma_ref[...] = total[:, :split]
    sumb_ref[...] = total[:, split:]


def halo_attention(scaling, bd, po, v, both, ds_ref):
    for g in range(po.shape[0]):
        values = jnp.concatenate([v[:, pair_cols(g)], po[g, TILE : 2 * TILE]], axis=0)
        both[g] = dot_nt(values, bd[g])
    row = lax.broadcasted_iota(jnp.int32, (TILE, 2 * TILE), 0)
    col = lax.broadcasted_iota(jnp.int32, (TILE, 2 * TILE), 1)
    same = (row == col) | (row + TILE == col)
    for g in range(po.shape[0]):
        delta = jnp.sum(jnp.where(same, both[g, TILE:], 0.0), axis=0, keepdims=True)
        ds = po[g, :TILE].astype(jnp.float32) * ((both[g, :TILE] - delta) * scaling)
        ds_ref[g] = ds.astype(jnp.bfloat16)


def own_kernel(
    scaling,
    acc,
    xa,
    xb,
    wot,
    qbd,
    pt,
    kt,
    v0,
    v1,
    v2,
    wqt,
    dq,
    dk_ref,
    dv_ref,
    base_ref,
    bd,
    dp,
    ds,
    turned,
):
    fill_diagonal(bd, wot, xb[...], acc)
    own_attention(scaling, bd, pt, v0, v1, v2, dp, ds)
    for g in range(pt.shape[0]):
        cols = pair_cols(g)
        dv_ref[:, cols] = dot_nn(pt[g, :TILE], bd[g])
        dk_ref[:, cols] = dot_nn(ds[g, :TILE], qbd[g])
    put_dq(ds, kt, turned, dq)
    base_ref[...] = xa[...].astype(jnp.float32) + dot_nn(dq[...], wqt[:, : xa.shape[1]])


def near_kernel(
    scaling,
    xfa,
    xa,
    xb,
    wot,
    qbd,
    po,
    v,
    dk_in,
    dv_in,
    after,
    acc_ref,
    dk_ref,
    dv_ref,
    bd,
    both,
    ds,
):
    x = jnp.concatenate([xa[...], xb[...]], axis=1)
    fill_diagonal(bd, wot, x, None)
    halo_attention(scaling, bd, po, v, both, ds)
    for g in range(po.shape[0]):
        cols = pair_cols(g)
        dv_ref[:, cols] = dv_in[:, cols] + dot_nn(po[g, :TILE], bd[g])
        dk_ref[:, cols] = dk_in[:, cols] + dot_nn(ds[g], qbd[g])
    acc_ref[...] = dot_nn(xfa[...], wot[: xfa.shape[1], :])


def far_kernel(
    scaling,
    acc,
    xb,
    wot,
    qbd,
    po,
    v,
    dk_in,
    dv_in,
    base,
    wkt,
    wvt,
    sum_ref,
    dk_ref,
    dv_ref,
    bd,
    both,
    ds,
):
    fill_diagonal(bd, wot, xb[...], acc)
    halo_attention(scaling, bd, po, v, both, ds)
    for g in range(po.shape[0]):
        cols = pair_cols(g)
        dv = dv_in[:, cols] + dot_nn(po[g, :TILE], bd[g])
        dk = dk_in[:, cols] + dot_nn(ds[g], qbd[g])
        dv_ref[:, cols] = dv.astype(jnp.bfloat16)
        dk_ref[:, cols] = dk.astype(jnp.bfloat16)
    part = pl.ds(0, sum_ref.shape[1])
    total = base[...] + project_pair(dk_ref, dv_ref, wkt, wvt, part)
    sum_ref[...] = total.astype(jnp.bfloat16)


def last_columns(dk, dv, dq, own_x, wqt, wkt, wvt):
    rest = own_x.shape[1]
    part = pl.ds(wqt.shape[1] - rest, rest)
    total = own_x[...].astype(jnp.float32) + dot_nn(dq[...], wqt[:, part])
    total = total + project_pair(dk, dv, wkt, wvt, part)
    return total.astype(jnp.bfloat16)


def rest_kernel(dk, dv, dq, own_x, wqt, wkt, wvt, sum_ref):
    sum_ref[...] = last_columns(dk, dv, dq, own_x, wqt, wkt, wvt)


def finish_kernel(dk, dv, dq, own_x, wqt, wkt, wvt, *refs):
    done_refs, out_ref = refs[:-1], refs[-1]
    position = lax.axis_index("pipe")
    split = done_refs[0].shape[1]
    out_ref[:, :split] = done_refs[-1][...]
    out_ref[:, split:] = last_columns(dk, dv, dq, own_x, wqt, wkt, wvt)
    count = len(done_refs) // 2
    for step in range(count):

        @pl.when(position == count - step)
        def _():
            out_ref[:, :split] = done_refs[2 * step][...]
            out_ref[:, split:] = done_refs[2 * step + 1][...]


def body(
    query_rows,
    key_rows,
    value_rows,
    query_weight,
    key_weight,
    value_weight,
    out_weight,
    upstream,
    window,
):
    sections = lax.axis_size("pipe")
    seq_size = lax.axis_size("seq")
    rows, width = query_rows.shape[1:]
    model = out_weight.shape[2]
    split = model // 2
    heads = width // HEAD_DIM
    pairs = heads // 2
    scaling = HEAD_DIM ** (-0.5)
    near_pairs = [(i, i ^ 1) for i in range(seq_size)]
    far_pairs = [(i, i + 1) for i in range(1, seq_size - 1, 2)]
    far_pairs = far_pairs + [(j, i) for i, j in far_pairs]

    def near(value):
        return lax.ppermute(value, "seq", near_pairs)

    def far(value):
        return lax.ppermute(value, "seq", far_pairs)

    def far_within(value, columns):
        moves = [(c * seq_size + i, c * seq_size + j) for c in columns for i, j in far_pairs]
        return lax.ppermute(value, ("pipe", "seq"), moves)

    def hop(value, source):
        return lax.ppermute(value, "pipe", [(source, source - 1)])

    vmem = pl.BlockSpec(memory_space=pltpu.VMEM)
    anywhere = pl.BlockSpec(memory_space=pl.ANY)
    bf16, f32 = jnp.bfloat16, jnp.float32
    weight = pltpu.VMEM((model, width), bf16)
    block = (pairs, 2 * TILE, 2 * HEAD_DIM)
    tile = pltpu.VMEM((rows, width), bf16)
    wide = pltpu.VMEM((rows, width), f32)
    whole = jax.ShapeDtypeStruct((rows, model), bf16)
    piece_a = jax.ShapeDtypeStruct((rows, split), bf16)
    piece_b = jax.ShapeDtypeStruct((rows, model - split), bf16)
    dp_scratch = pltpu.VMEM((pairs, 3 * TILE, 2 * TILE), f32)
    turned_scratch = pltpu.VMEM((heads, HEAD_DIM, TILE), f32)
    halo_scratch = [
        pltpu.VMEM(block, bf16),
        pltpu.VMEM(block, f32),
        pltpu.VMEM((pairs, TILE, 2 * TILE), bf16),
    ]
    diagonal = pltpu.VMEM(block, bf16)

    def call(kernel, name, ins, outs, scratch=(), limit=12, cost=0):
        single = not isinstance(outs, list)
        estimate = pl.CostEstimate(flops=cost, bytes_accessed=0, transcendentals=0)
        return pl.pallas_call(
            kernel,
            in_specs=ins,
            out_specs=vmem if single else [vmem] * len(outs),
            out_shape=outs,
            scratch_shapes=list(scratch),
            compiler_params=pltpu.CompilerParams(vmem_limit_bytes=limit * MIB),
            cost_estimate=estimate if cost else None,
            name=name,
        )

    def mark(*values, cost=10**10):
        token = pltpu.VMEM((8, 128), f32)
        return call(mark_kernel, "mark", [anywhere] * len(values), token, cost=cost)(*values)

    k2 = far(key_rows[0])
    v2 = far(value_rows[0])
    k1 = near(key_rows[0])
    wot, wkt, wvt, wqt, q, k, v, x, qbd, keep = call(
        prep_kernel,
        "prep",
        [anywhere] * 9,
        [
            weight,
            weight,
            weight,
            weight,
            tile,
            tile,
            tile,
            tile,
            diagonal,
            pltpu.VMEM((2, pairs, 8, 2 * TILE), jnp.int32),
        ],
        [
            pltpu.VMEM((4, model, width), bf16),
            pltpu.SMEM((window.shape[0], 2, heads), jnp.int32),
            pltpu.SemaphoreType.DMA((21,)),
        ],
        36,
    )(
        out_weight[0],
        key_weight[0],
        value_weight[0],
        query_weight[0],
        query_rows[0],
        key_rows[0],
        value_rows[0],
        upstream,
        jnp.transpose(window, (0, 2, 1)),
    )
    v1 = near(v)
    pt, kt = call(
        functools.partial(prob_kernel, scaling),
        "prob",
        [vmem] * 5 + [anywhere],
        [
            pltpu.VMEM((pairs, 3 * TILE, 2 * rows), bf16),
            pltpu.VMEM((heads, HEAD_DIM, 3 * TILE), bf16),
        ],
        [dp_scratch],
    )(keep, qbd, k, k1, k2, mark(k1, k2))

    to_far, ds, bd = call(
        functools.partial(first_far_kernel, sections - 1, scaling),
        "first_far",
        [vmem] * 9 + [anywhere],
        [whole, pltpu.VMEM((pairs, 3 * TILE, 2 * rows), bf16), diagonal],
        [tile, tile, dp_scratch],
    )(x, wot, qbd, pt, v, v1, v2, wkt, wvt, mark(v2, pt))
    from_far = far(to_far)
    to_near = call(
        functools.partial(first_near_kernel, sections - 1), "first_near", [vmem] * 6, whole, [tile, tile])(
        ds, bd, qbd, pt, wkt, wvt
    )
    from_near = near(to_near)
    packet = pltpu.VMEM((pairs, 3 * TILE, 2 * HEAD_DIM), bf16)
    po_to_near, po_to_far = call(out_kernel, "out", [vmem] * 5 + [anywhere], [packet, packet])(
        pt, q, v, v1, v2, to_near
    )
    pof = far_within(po_to_far, range(sections - 1))
    pon = near(po_to_near)
    turn = call(turn_kernel, "turn", [vmem], diagonal)
    qbdn, qbdf = turn(pon), turn(pof)
    base = call(
        functools.partial(first_own_kernel, sections - 1),
        "first_own",
        [vmem] * 9 + [anywhere],
        wide,
        [tile, tile, tile, turned_scratch],
    )(x, ds, bd, qbd, pt, kt, wqt, wkt, wvt, po_to_far)
    done_a, done_b = call(
        first_sum_kernel, "first_sum", [vmem] * 3 + [anywhere], [piece_a, piece_b]
    )(base, from_near, from_far, mark(from_far))
    done = [done_a, done_b]

    for step in range(1, sections):
        source = sections - step
        xa = hop(done_a, source)
        xb = hop(done_b, source)
        acc, xa_copy = call(
            begin_kernel, "begin", [vmem] * 2 + [anywhere], [wide, piece_a]
        )(xa, wot, qbdn)
        xfa, xfb = far(xa_copy), far(xb)
        xna, xnb = near(xa_copy), near(xb)
        dq, dk, dv, base = call(
            functools.partial(own_kernel, scaling),
            "own",
            [vmem] * 11,
            [tile, wide, wide, pltpu.VMEM((rows, split), f32)],
            [
                pltpu.VMEM(block, bf16),
                dp_scratch,
                pltpu.VMEM((pairs, 3 * TILE, 2 * TILE), bf16),
                turned_scratch,
            ],
        )(acc, xa, xb, wot, qbd, pt, kt, v, v1, v2, wqt)
        acc, dk, dv = call(
            functools.partial(near_kernel, scaling),
            "near",
            [vmem] * 9 + [anywhere],
            [wide, wide, wide],
            halo_scratch,
        )(xfa, xna, xnb, wot, qbdn, pon, v, dk, dv, mark(xfa, xna, cost=10**8))
        done_a, dk, dv = call(
            functools.partial(far_kernel, scaling),
            "far",
            [vmem] * 11,
            [piece_a, tile, tile],
            halo_scratch,
        )(acc, xfb, wot, qbdf, pof, v, dk, dv, base, wkt, wvt)
        rest_in = (dk, dv, dq, xb, wqt, wkt, wvt)
        if step < sections - 1:
            done_b = call(rest_kernel, "rest", [vmem] * 7, piece_b)(*rest_in)
            done += [done_a, done_b]
    out = call(
        finish_kernel,
        "finish",
        [vmem] * (8 + len(done)),
        jax.ShapeDtypeStruct((rows, model), bf16),
    )(*rest_in, *done, done_a)
    return out[None]


def solution(mesh):
    in_specs = (
        P("pipe", "seq", None),
        P("pipe", "seq", None),
        P("pipe", "seq", None),
        P("pipe", None, None),
        P("pipe", None, None),
        P("pipe", None, None),
        P("pipe", None, None),
        P("seq", None),
        P(),
    )
    out_specs = P("pipe", "seq", None)
    return jax.shard_map(body, mesh=mesh, in_specs=in_specs, out_specs=out_specs, check_vma=False)
```

```python
import functools

import jax
import jax.numpy as jnp
from jax import lax
from jax.experimental import pallas as pl
from jax.experimental.pallas import tpu as pltpu
from jax.sharding import PartitionSpec as P

HEAD_DIM = 128
TILE = 128
MIB = 1 << 20


def dot_nt(a, b):
    return lax.dot_general(a, b, (((1,), (1,)), ((), ())), preferred_element_type=jnp.float32)


def dot_nn(a, b):
    return lax.dot_general(a, b, (((1,), (0,)), ((), ())), preferred_element_type=jnp.float32)


def pair_cols(g):
    return pl.ds(g * 2 * HEAD_DIM, 2 * HEAD_DIM)


def put_diagonal(target, g, value):
    target[g, pl.ds(0, TILE), pl.ds(0, HEAD_DIM)] = value[:, :HEAD_DIM]
    target[g, pl.ds(TILE, TILE), pl.ds(HEAD_DIM, HEAD_DIM)] = value[:, HEAD_DIM:]


def prep_kernel(
    wo_hbm,
    wk_hbm,
    wv_hbm,
    wq_hbm,
    q_hbm,
    k_hbm,
    v_hbm,
    x_hbm,
    window,
    wot,
    wkt,
    wvt,
    wqt,
    q,
    k,
    v,
    x,
    qbd,
    keep,
    raw,
    flags,
    sems,
):
    groups = 4
    rows = raw.shape[1] // groups
    small = [
        pltpu.make_async_copy(src, dst, sems.at[n])
        for n, (src, dst) in enumerate(((q_hbm, q), (k_hbm, k), (v_hbm, v), (x_hbm, x)))
    ]
    sources = (wo_hbm, wk_hbm, wv_hbm, wq_hbm)

    def large(n, g):
        part = pl.ds(g * rows, rows)
        return pltpu.make_async_copy(
            sources[n].at[part], raw.at[n, part], sems.at[4 + n * groups + g]
        )

    window_copy = pltpu.make_async_copy(window, flags, sems.at[20])
    window_copy.start()
    for copy in small:
        copy.start()
    for n in range(len(sources)):
        for g in range(groups):
            large(n, g).start()
    qbd[...] = jnp.zeros_like(qbd)
    for copy in small:
        copy.wait()
    for g in range(qbd.shape[0]):
        put_diagonal(qbd, g, q[:, pair_cols(g)])
    for n, dst in enumerate((wot, wkt, wvt, wqt)):

        @pl.loop(0, groups)
        def _(g, n=n, dst=dst):
            start = pl.multiple_of(g * rows, rows)
            large(n, g).wait()
            for r in range(0, rows, TILE):
                part = pl.ds(start + r, TILE)
                dst[:, part] = raw[n, part, :].T
    window_copy.wait()
    tile = lax.axis_index("seq")
    odd = lax.rem(tile, 2)
    lane = lax.broadcasted_iota(jnp.int32, keep.shape[2:], 1)
    for b, side in enumerate((1 - odd, odd)):
        for g in range(keep.shape[1]):
            keep[b, g] = jnp.where(
                lane < TILE, flags[tile, side, 2 * g], flags[tile, side, 2 * g + 1]
            )


def prob_kernel(scaling, keep, qbd, k0, k1, k2, pt_ref, kt_ref, scores):
    pairs = pt_ref.shape[0]
    for g in range(pairs):
        cols = pair_cols(g)
        keys = jnp.concatenate([k0[:, cols], k1[:, cols], k2[:, cols]], axis=0)
        scores[g] = dot_nt(keys, qbd[g])
        for b, k_ref in enumerate((k0, k1, k2)):
            for n in range(2):
                h = 2 * g + n
                part = k_ref[:, pl.ds(h * HEAD_DIM, HEAD_DIM)]
                kt_ref[h, :, pl.ds(b * TILE, TILE)] = part.T
    for g in range(pairs):
        parts = []
        for b in range(3):
            s = scaling * scores[g, pl.ds(b * TILE, TILE)]
            if b > 0:
                s = jnp.where(keep[b - 1, g, 0:1] > 0, s, -jnp.inf)
            parts.append(s)
        top = jnp.maximum(jnp.maximum(parts[0], parts[1]), parts[2])
        top = jnp.max(top, axis=0, keepdims=True)
        weights = [jnp.exp(s - top) for s in parts]
        total = jnp.sum(weights[0] + weights[1] + weights[2], axis=0, keepdims=True)
        scale = 1.0 / total
        for b, w in enumerate(weights):
            pt_ref[g, pl.ds(b * TILE, TILE), :] = (w * scale).astype(jnp.bfloat16)


def out_kernel(pt, q, v0, v1, v2, after, pon_ref, pof_ref):
    for g in range(pt.shape[0]):
        pon_ref[g, :TILE] = pt[g, TILE : 2 * TILE]
        pof_ref[g, :TILE] = pt[g, 2 * TILE :]
        for n in range(2):
            cols = pl.ds((2 * g + n) * HEAD_DIM, HEAD_DIM)
            lanes = pl.ds(n * HEAD_DIM, HEAD_DIM)
            values = jnp.concatenate([v0[:, cols], v1[:, cols], v2[:, cols]], axis=0)
            out = dot_nn(pt[g, :, lanes].T, values).astype(jnp.bfloat16)
            pon_ref[g, pl.ds(TILE, TILE), lanes] = out
            pof_ref[g, pl.ds(TILE, TILE), lanes] = out
        queries = q[:, pair_cols(g)]
        pon_ref[g, 2 * TILE :] = queries
        pof_ref[g, 2 * TILE :] = queries


def turn_kernel(po, qbd):
    qbd[...] = jnp.zeros_like(qbd)
    for g in range(qbd.shape[0]):
        put_diagonal(qbd, g, po[g, 2 * TILE :])


def inside(value):
    tile = lax.axis_index("seq")
    edge = (tile == 0) | (tile == lax.axis_size("seq") - 1)
    return jnp.where(edge, jnp.zeros_like(value), value)


def clean_kernel(value, before, out_ref):
    out_ref[...] = inside(value[...])


def mark_kernel(*refs):
    refs[-1][...] = jnp.zeros_like(refs[-1])


def begin_kernel(column, xa_ref, wot, after, acc_ref, copy_ref):
    @pl.when(lax.axis_index("pipe") == column)
    def _():
        x = xa_ref[...]
        copy_ref[...] = x
        acc_ref[...] = dot_nn(x, wot[: x.shape[1], :])


def fill_diagonal(bd, wot, x, acc_ref):
    bd[...] = jnp.zeros_like(bd)
    start = wot.shape[0] - x.shape[1]
    for g in range(bd.shape[0]):
        cols = pair_cols(g)
        d_out = dot_nn(x, wot[start:, cols])
        if acc_ref is not None:
            d_out = acc_ref[:, cols] + d_out
        put_diagonal(bd, g, d_out.astype(jnp.bfloat16))


def own_attention(scaling, bd, pt, v0, v1, v2, dp, ds_ref):
    for g in range(pt.shape[0]):
        cols = pair_cols(g)
        values = jnp.concatenate([v0[:, cols], v1[:, cols], v2[:, cols]], axis=0)
        dp[g] = dot_nt(values, bd[g])
    for g in range(pt.shape[0]):
        pf = pt[g].astype(jnp.float32)
        delta = jnp.sum(pf * dp[g], axis=0, keepdims=True)
        ds_ref[g] = (pf * ((dp[g] - delta) * scaling)).astype(jnp.bfloat16)


def put_dq(ds, kt, turned, dq):
    for h in range(kt.shape[0]):
        turned[h] = dot_nn(kt[h], ds[h // 2, :, pl.ds((h % 2) * TILE, TILE)])
    for h in range(kt.shape[0]):
        dq[:, pl.ds(h * HEAD_DIM, HEAD_DIM)] = turned[h].T.astype(jnp.bfloat16)


def project_pair(dk, dv, wkt, wvt, part):
    return dot_nn(dk[...], wkt[:, part]) + dot_nn(dv[...], wvt[:, part])


def first_far_kernel(
    last, scaling, x, wot, qbd, pt, v0, v1, v2, wkt, wvt, far_ref, ds_ref, bd, dk, dv, dp
):
    @pl.when(lax.axis_index("pipe") == last)
    def _():
        fill_diagonal(bd, wot, x[...], None)
        own_attention(scaling, bd, pt, v0, v1, v2, dp, ds_ref)
        for g in range(pt.shape[0]):
            cols = pair_cols(g)
            dv[:, cols] = dot_nn(pt[g, 2 * TILE :], bd[g]).astype(jnp.bfloat16)
            dk[:, cols] = dot_nn(ds_ref[g, 2 * TILE :], qbd[g]).astype(jnp.bfloat16)
        far_ref[...] = project_pair(dk, dv, wkt, wvt, slice(None)).astype(jnp.bfloat16)


def first_near_kernel(last, ds_ref, bd, qbd, pt, wkt, wvt, near_ref, dk, dv):
    @pl.when(lax.axis_index("pipe") == last)
    def _():
        for g in range(pt.shape[0]):
            cols = pair_cols(g)
            dv[:, cols] = dot_nn(pt[g, TILE : 2 * TILE], bd[g]).astype(jnp.bfloat16)
            dk[:, cols] = dot_nn(ds_ref[g, TILE : 2 * TILE], qbd[g]).astype(jnp.bfloat16)
        near_ref[...] = project_pair(dk, dv, wkt, wvt, slice(None)).astype(jnp.bfloat16)


def first_own_kernel(
    last, x, ds_ref, bd, qbd, pt, kt, wqt, wkt, wvt, after, base_ref, dq, dk, dv, turned
):
    @pl.when(lax.axis_index("pipe") == last)
    def _():
        for g in range(pt.shape[0]):
            cols = pair_cols(g)
            dv[:, cols] = dot_nn(pt[g, :TILE], bd[g]).astype(jnp.bfloat16)
            dk[:, cols] = dot_nn(ds_ref[g, :TILE], qbd[g]).astype(jnp.bfloat16)
        put_dq(ds_ref, kt, turned, dq)
        base = project_pair(dk, dv, wkt, wvt, slice(None)) + dot_nn(dq[...], wqt[...])
        base_ref[...] = base + x[...].astype(jnp.float32)


def first_sum_kernel(base, near, far, after, suma_ref, sumb_ref):
    total = base[...] + near[...].astype(jnp.float32) + inside(far[...]).astype(jnp.float32)
    total = total.astype(jnp.bfloat16)
    split = suma_ref.shape[1]
    suma_ref[...] = total[:, :split]
    sumb_ref[...] = total[:, split:]


def halo_attention(scaling, bd, po, v, both, ds_ref):
    for g in range(po.shape[0]):
        values = jnp.concatenate([v[:, pair_cols(g)], po[g, TILE : 2 * TILE]], axis=0)
        both[g] = dot_nt(values, bd[g])
    row = lax.broadcasted_iota(jnp.int32, (TILE, 2 * TILE), 0)
    col = lax.broadcasted_iota(jnp.int32, (TILE, 2 * TILE), 1)
    same = (row == col) | (row + TILE == col)
    for g in range(po.shape[0]):
        delta = jnp.sum(jnp.where(same, both[g, TILE:], 0.0), axis=0, keepdims=True)
        ds = po[g, :TILE].astype(jnp.float32) * ((both[g, :TILE] - delta) * scaling)
        ds_ref[g] = ds.astype(jnp.bfloat16)


def own_kernel(
    column,
    scaling,
    acc,
    xa,
    xb,
    wot,
    qbd,
    pt,
    kt,
    v0,
    v1,
    v2,
    wqt,
    dq,
    dk_ref,
    dv_ref,
    base_ref,
    bd,
    dp,
    ds,
    turned,
):
    @pl.when(lax.axis_index("pipe") == column)
    def _():
        fill_diagonal(bd, wot, xb[...], acc)
        own_attention(scaling, bd, pt, v0, v1, v2, dp, ds)
        for g in range(pt.shape[0]):
            cols = pair_cols(g)
            dv_ref[:, cols] = dot_nn(pt[g, :TILE], bd[g])
            dk_ref[:, cols] = dot_nn(ds[g, :TILE], qbd[g])
        put_dq(ds, kt, turned, dq)
        base_ref[...] = xa[...].astype(jnp.float32) + dot_nn(dq[...], wqt[:, : xa.shape[1]])


def near_kernel(
    column,
    scaling,
    xfa,
    xa,
    xb,
    wot,
    qbd,
    po,
    v,
    dk_in,
    dv_in,
    after,
    acc_ref,
    dk_ref,
    dv_ref,
    bd,
    both,
    ds,
):
    @pl.when(lax.axis_index("pipe") == column)
    def _():
        x = jnp.concatenate([xa[...], xb[...]], axis=1)
        fill_diagonal(bd, wot, x, None)
        halo_attention(scaling, bd, po, v, both, ds)
        for g in range(po.shape[0]):
            cols = pair_cols(g)
            dv_ref[:, cols] = dv_in[:, cols] + dot_nn(po[g, :TILE], bd[g])
            dk_ref[:, cols] = dk_in[:, cols] + dot_nn(ds[g], qbd[g])
        acc_ref[...] = dot_nn(inside(xfa[...]), wot[: xfa.shape[1], :])


def far_kernel(
    column,
    scaling,
    acc,
    xb,
    wot,
    qbd,
    po,
    v,
    dk_in,
    dv_in,
    base,
    wkt,
    wvt,
    sum_ref,
    dk_ref,
    dv_ref,
    bd,
    both,
    ds,
):
    @pl.when(lax.axis_index("pipe") == column)
    def _():
        fill_diagonal(bd, wot, inside(xb[...]), acc)
        halo_attention(scaling, bd, po, v, both, ds)
        for g in range(po.shape[0]):
            cols = pair_cols(g)
            dv = dv_in[:, cols] + dot_nn(po[g, :TILE], bd[g])
            dk = dk_in[:, cols] + dot_nn(ds[g], qbd[g])
            dv_ref[:, cols] = dv.astype(jnp.bfloat16)
            dk_ref[:, cols] = dk.astype(jnp.bfloat16)
        part = pl.ds(0, sum_ref.shape[1])
        total = base[...] + project_pair(dk_ref, dv_ref, wkt, wvt, part)
        sum_ref[...] = total.astype(jnp.bfloat16)


def last_columns(dk, dv, dq, own_x, wqt, wkt, wvt):
    rest = own_x.shape[1]
    part = pl.ds(wqt.shape[1] - rest, rest)
    total = own_x[...].astype(jnp.float32) + dot_nn(dq[...], wqt[:, part])
    total = total + project_pair(dk, dv, wkt, wvt, part)
    return total.astype(jnp.bfloat16)


def rest_kernel(column, dk, dv, dq, own_x, wqt, wkt, wvt, sum_ref):
    @pl.when(lax.axis_index("pipe") == column)
    def _():
        sum_ref[...] = last_columns(dk, dv, dq, own_x, wqt, wkt, wvt)


def finish_kernel(dk, dv, dq, own_x, wqt, wkt, wvt, *refs):
    done_refs, out_ref = refs[:-1], refs[-1]
    position = lax.axis_index("pipe")
    split = done_refs[0].shape[1]
    out_ref[:, :split] = done_refs[-1][...]
    out_ref[:, split:] = last_columns(dk, dv, dq, own_x, wqt, wkt, wvt)
    count = len(done_refs) // 2
    for step in range(count):

        @pl.when(position == count - step)
        def _():
            out_ref[:, :split] = done_refs[2 * step][...]
            out_ref[:, split:] = done_refs[2 * step + 1][...]


def body(
    query_rows,
    key_rows,
    value_rows,
    query_weight,
    key_weight,
    value_weight,
    out_weight,
    upstream,
    window,
):
    sections = lax.axis_size("pipe")
    seq_size = lax.axis_size("seq")
    rows, width = query_rows.shape[1:]
    model = out_weight.shape[2]
    split = model // 2
    heads = width // HEAD_DIM
    pairs = heads // 2
    scaling = HEAD_DIM ** (-0.5)
    near_pairs = [(i, i ^ 1) for i in range(seq_size)]
    far_pairs = [(i, i + 1) for i in range(1, seq_size - 1, 2)]
    far_pairs = far_pairs + [(j, i) for i, j in far_pairs]

    def near(value):
        return lax.ppermute(value, "seq", near_pairs)

    def spread(pairs_of):
        tiles = range(seq_size)
        return [
            (c * seq_size + i, d * seq_size + j)
            for c in range(sections)
            for i in tiles
            for d, j in [pairs_of(c, i)]
        ]

    def far(value):
        partner = dict(far_pairs)

        def pairs_of(c, i):
            return (c, partner[i]) if i in partner else ((c + sections // 2) % sections, i)

        return lax.ppermute(value, ("pipe", "seq"), spread(pairs_of))

    def far_within(value, columns):
        moves = [(c * seq_size + i, c * seq_size + j) for c in columns for i, j in far_pairs]
        return lax.ppermute(value, ("pipe", "seq"), moves)

    def hop(value, source):
        def pairs_of(c, i):
            return (2 * source - 1 - c) % sections, i

        return lax.ppermute(value, ("pipe", "seq"), spread(pairs_of))

    vmem = pl.BlockSpec(memory_space=pltpu.VMEM)
    anywhere = pl.BlockSpec(memory_space=pl.ANY)
    bf16, f32 = jnp.bfloat16, jnp.float32
    weight = pltpu.VMEM((model, width), bf16)
    block = (pairs, 2 * TILE, 2 * HEAD_DIM)
    tile = pltpu.VMEM((rows, width), bf16)
    wide = pltpu.VMEM((rows, width), f32)
    whole = jax.ShapeDtypeStruct((rows, model), bf16)
    piece_a = jax.ShapeDtypeStruct((rows, split), bf16)
    piece_b = jax.ShapeDtypeStruct((rows, model - split), bf16)
    dp_scratch = pltpu.VMEM((pairs, 3 * TILE, 2 * TILE), f32)
    turned_scratch = pltpu.VMEM((heads, HEAD_DIM, TILE), f32)
    halo_scratch = [
        pltpu.VMEM(block, bf16),
        pltpu.VMEM(block, f32),
        pltpu.VMEM((pairs, TILE, 2 * TILE), bf16),
    ]
    diagonal = pltpu.VMEM(block, bf16)

    def call(kernel, name, ins, outs, scratch=(), limit=12, cost=0):
        single = not isinstance(outs, list)
        estimate = pl.CostEstimate(flops=cost, bytes_accessed=0, transcendentals=0)
        return pl.pallas_call(
            kernel,
            in_specs=ins,
            out_specs=vmem if single else [vmem] * len(outs),
            out_shape=outs,
            scratch_shapes=list(scratch),
            compiler_params=pltpu.CompilerParams(vmem_limit_bytes=limit * MIB),
            cost_estimate=estimate if cost else None,
            name=name,
        )

    def mark(*values, cost=10**10):
        token = pltpu.VMEM((8, 128), f32)
        return call(mark_kernel, "mark", [anywhere] * len(values), token, cost=cost)(*values)

    k2 = far(key_rows[0])
    v2 = far(value_rows[0])
    k1 = near(key_rows[0])
    wot, wkt, wvt, wqt, q, k, v, x, qbd, keep = call(
        prep_kernel,
        "prep",
        [anywhere] * 9,
        [
            weight,
            weight,
            weight,
            weight,
            tile,
            tile,
            tile,
            tile,
            diagonal,
            pltpu.VMEM((2, pairs, 8, 2 * TILE), jnp.int32),
        ],
        [
            pltpu.VMEM((4, model, width), bf16),
            pltpu.SMEM((window.shape[0], 2, heads), jnp.int32),
            pltpu.SemaphoreType.DMA((21,)),
        ],
        36,
    )(
        out_weight[0],
        key_weight[0],
        value_weight[0],
        query_weight[0],
        query_rows[0],
        key_rows[0],
        value_rows[0],
        upstream,
        jnp.transpose(window, (0, 2, 1)),
    )
    v1 = near(v)
    clean = call(clean_kernel, "clean", [vmem, anywhere], tile, cost=10**10)
    pt, kt = call(
        functools.partial(prob_kernel, scaling),
        "prob",
        [vmem] * 5,
        [
            pltpu.VMEM((pairs, 3 * TILE, 2 * rows), bf16),
            pltpu.VMEM((heads, HEAD_DIM, 3 * TILE), bf16),
        ],
        [dp_scratch],
    )(keep, qbd, k, k1, clean(k2, k1))

    v2 = clean(v2, pt)
    to_far, ds, bd = call(
        functools.partial(first_far_kernel, sections - 1, scaling),
        "first_far",
        [vmem] * 9,
        [whole, pltpu.VMEM((pairs, 3 * TILE, 2 * rows), bf16), diagonal],
        [tile, tile, dp_scratch],
    )(x, wot, qbd, pt, v, v1, v2, wkt, wvt)
    from_far = far(to_far)
    to_near = call(
        functools.partial(first_near_kernel, sections - 1), "first_near", [vmem] * 6, whole, [tile, tile])(
        ds, bd, qbd, pt, wkt, wvt
    )
    from_near = near(to_near)
    packet = pltpu.VMEM((pairs, 3 * TILE, 2 * HEAD_DIM), bf16)
    po_to_near, po_to_far = call(out_kernel, "out", [vmem] * 5 + [anywhere], [packet, packet])(
        pt, q, v, v1, v2, to_near
    )
    pof = far_within(po_to_far, range(sections - 1))
    pon = near(po_to_near)
    turn = call(turn_kernel, "turn", [vmem], diagonal)
    qbdn, qbdf = turn(pon), turn(pof)
    base = call(
        functools.partial(first_own_kernel, sections - 1),
        "first_own",
        [vmem] * 9 + [anywhere],
        wide,
        [tile, tile, tile, turned_scratch],
    )(x, ds, bd, qbd, pt, kt, wqt, wkt, wvt, po_to_far)
    done_a, done_b = call(
        first_sum_kernel, "first_sum", [vmem] * 3 + [anywhere], [piece_a, piece_b]
    )(base, from_near, from_far, mark(from_far))
    done = [done_a, done_b]

    for step in range(1, sections):
        source = sections - step
        xa = hop(done_a, source)
        xb = hop(done_b, source)
        acc, xa_copy = call(
            functools.partial(begin_kernel, source - 1), "begin", [vmem] * 2 + [anywhere], [wide, piece_a]
        )(xa, wot, qbdn)
        xfa, xfb = far(xa_copy), far(xb)
        xna, xnb = near(xa_copy), near(xb)
        dq, dk, dv, base = call(
            functools.partial(own_kernel, source - 1, scaling),
            "own",
            [vmem] * 11,
            [tile, wide, wide, pltpu.VMEM((rows, split), f32)],
            [
                pltpu.VMEM(block, bf16),
                dp_scratch,
                pltpu.VMEM((pairs, 3 * TILE, 2 * TILE), bf16),
                turned_scratch,
            ],
        )(acc, xa, xb, wot, qbd, pt, kt, v, v1, v2, wqt)
        acc, dk, dv = call(
            functools.partial(near_kernel, source - 1, scaling),
            "near",
            [vmem] * 9 + [anywhere],
            [wide, wide, wide],
            halo_scratch,
        )(xfa, xna, xnb, wot, qbdn, pon, v, dk, dv, mark(xfa, xna, cost=10**8))
        done_a, dk, dv = call(
            functools.partial(far_kernel, source - 1, scaling),
            "far",
            [vmem] * 11,
            [piece_a, tile, tile],
            halo_scratch,
        )(acc, xfb, wot, qbdf, pof, v, dk, dv, base, wkt, wvt)
        rest_in = (dk, dv, dq, xb, wqt, wkt, wvt)
        if step < sections - 1:
            done_b = call(
                functools.partial(rest_kernel, source - 1), "rest", [vmem] * 7, piece_b
            )(*rest_in)
            done += [done_a, done_b]
    out = call(
        finish_kernel,
        "finish",
        [vmem] * (8 + len(done)),
        jax.ShapeDtypeStruct((rows, model), bf16),
    )(*rest_in, *done, done_a)
    return out[None]


def solution(mesh):
    in_specs = (
        P("pipe", "seq", None),
        P("pipe", "seq", None),
        P("pipe", "seq", None),
        P("pipe", None, None),
        P("pipe", None, None),
        P("pipe", None, None),
        P("pipe", None, None),
        P("seq", None),
        P(),
    )
    out_specs = P("pipe", "seq", None)
    return jax.shard_map(body, mesh=mesh, in_specs=in_specs, out_specs=out_specs, check_vma=False)
```

```python
import functools

import jax
import jax.numpy as jnp
from jax import lax
from jax.experimental import pallas as pl
from jax.experimental.pallas import tpu as pltpu
from jax.sharding import PartitionSpec as P

HEAD_DIM = 128
TILE = 128
MIB = 1 << 20


def dot_nt(a, b):
    return lax.dot_general(a, b, (((1,), (1,)), ((), ())), preferred_element_type=jnp.float32)


def dot_nn(a, b):
    return lax.dot_general(a, b, (((1,), (0,)), ((), ())), preferred_element_type=jnp.float32)


def pair_cols(g):
    return pl.ds(g * 2 * HEAD_DIM, 2 * HEAD_DIM)


def put_diagonal(target, g, value):
    target[g, pl.ds(0, TILE), pl.ds(0, HEAD_DIM)] = value[:, :HEAD_DIM]
    target[g, pl.ds(TILE, TILE), pl.ds(HEAD_DIM, HEAD_DIM)] = value[:, HEAD_DIM:]


def prep_kernel(
    wo_hbm,
    wk_hbm,
    wv_hbm,
    wq_hbm,
    q_hbm,
    k_hbm,
    v_hbm,
    x_hbm,
    window,
    wot,
    wkt,
    wvt,
    wqt,
    q,
    k,
    v,
    x,
    qbd,
    keep,
    raw,
    flags,
    sems,
):
    groups = 4
    rows = raw.shape[1] // groups
    small = [
        pltpu.make_async_copy(src, dst, sems.at[n])
        for n, (src, dst) in enumerate(((q_hbm, q), (k_hbm, k), (v_hbm, v), (x_hbm, x)))
    ]
    sources = (wo_hbm, wk_hbm, wv_hbm, wq_hbm)

    def large(n, g):
        part = pl.ds(g * rows, rows)
        return pltpu.make_async_copy(
            sources[n].at[part], raw.at[n, part], sems.at[4 + n * groups + g]
        )

    window_copy = pltpu.make_async_copy(window, flags, sems.at[20])
    window_copy.start()
    for copy in small:
        copy.start()
    for n in range(len(sources)):
        for g in range(groups):
            large(n, g).start()
    qbd[...] = jnp.zeros_like(qbd)
    for copy in small:
        copy.wait()
    for g in range(qbd.shape[0]):
        put_diagonal(qbd, g, q[:, pair_cols(g)])
    for n, dst in enumerate((wot, wkt, wvt, wqt)):

        @pl.loop(0, groups)
        def _(g, n=n, dst=dst):
            start = pl.multiple_of(g * rows, rows)
            large(n, g).wait()
            for r in range(0, rows, TILE):
                part = pl.ds(start + r, TILE)
                dst[:, part] = raw[n, part, :].T
    window_copy.wait()
    tile = lax.axis_index("seq")
    odd = lax.rem(tile, 2)
    lane = lax.broadcasted_iota(jnp.int32, keep.shape[2:], 1)
    for b, side in enumerate((1 - odd, odd)):
        for g in range(keep.shape[1]):
            keep[b, g] = jnp.where(
                lane < TILE, flags[tile, side, 2 * g], flags[tile, side, 2 * g + 1]
            )


def prob_kernel(scaling, keep, qbd, k0, k1, k2, pt_ref, kt_ref, scores):
    pairs = pt_ref.shape[0]
    for g in range(pairs):
        cols = pair_cols(g)
        keys = jnp.concatenate([k0[:, cols], k1[:, cols], k2[:, cols]], axis=0)
        scores[g] = dot_nt(keys, qbd[g])
        for b, k_ref in enumerate((k0, k1, k2)):
            for n in range(2):
                h = 2 * g + n
                part = k_ref[:, pl.ds(h * HEAD_DIM, HEAD_DIM)]
                kt_ref[h, :, pl.ds(b * TILE, TILE)] = part.T
    for g in range(pairs):
        parts = []
        for b in range(3):
            s = scaling * scores[g, pl.ds(b * TILE, TILE)]
            if b > 0:
                s = jnp.where(keep[b - 1, g, 0:1] > 0, s, -jnp.inf)
            parts.append(s)
        top = jnp.maximum(jnp.maximum(parts[0], parts[1]), parts[2])
        top = jnp.max(top, axis=0, keepdims=True)
        weights = [jnp.exp(s - top) for s in parts]
        total = jnp.sum(weights[0] + weights[1] + weights[2], axis=0, keepdims=True)
        scale = 1.0 / total
        for b, w in enumerate(weights):
            pt_ref[g, pl.ds(b * TILE, TILE), :] = (w * scale).astype(jnp.bfloat16)


def out_kernel(last, pt, q, v0, v1, v2, after, pon_ref, pof_ref):
    @pl.when(lax.axis_index("pipe") < last)
    def _():
        for g in range(pt.shape[0]):
            pon_ref[g, :TILE] = pt[g, TILE : 2 * TILE]
            pof_ref[g, :TILE] = pt[g, 2 * TILE :]
            for n in range(2):
                cols = pl.ds((2 * g + n) * HEAD_DIM, HEAD_DIM)
                lanes = pl.ds(n * HEAD_DIM, HEAD_DIM)
                values = jnp.concatenate([v0[:, cols], v1[:, cols], v2[:, cols]], axis=0)
                out = dot_nn(pt[g, :, lanes].T, values).astype(jnp.bfloat16)
                pon_ref[g, pl.ds(TILE, TILE), lanes] = out
                pof_ref[g, pl.ds(TILE, TILE), lanes] = out
            queries = q[:, pair_cols(g)]
            pon_ref[g, 2 * TILE :] = queries
            pof_ref[g, 2 * TILE :] = queries


def turn_kernel(po, qbd):
    qbd[...] = jnp.zeros_like(qbd)
    for g in range(qbd.shape[0]):
        put_diagonal(qbd, g, po[g, 2 * TILE :])


def inside(value):
    tile = lax.axis_index("seq")
    edge = (tile == 0) | (tile == lax.axis_size("seq") - 1)
    return jnp.where(edge, jnp.zeros_like(value), value)


def clean_kernel(value, *refs):
    refs[-1][...] = inside(value[...])


def mark_kernel(*refs):
    refs[-1][...] = jnp.zeros_like(refs[-1])


def begin_kernel(column, xa_ref, wot, after, acc_ref, copy_ref):
    @pl.when(lax.axis_index("pipe") == column)
    def _():
        x = xa_ref[...]
        copy_ref[...] = x
        acc_ref[...] = dot_nn(x, wot[: x.shape[1], :])


def fill_diagonal(bd, wot, x, acc_ref):
    bd[...] = jnp.zeros_like(bd)
    start = wot.shape[0] - x.shape[1]
    for g in range(bd.shape[0]):
        cols = pair_cols(g)
        d_out = dot_nn(x, wot[start:, cols])
        if acc_ref is not None:
            d_out = acc_ref[:, cols] + d_out
        put_diagonal(bd, g, d_out.astype(jnp.bfloat16))


def own_attention(scaling, bd, pt, v0, v1, v2, dp, ds_ref):
    for g in range(pt.shape[0]):
        cols = pair_cols(g)
        values = jnp.concatenate([v0[:, cols], v1[:, cols], v2[:, cols]], axis=0)
        dp[g] = dot_nt(values, bd[g])
    for g in range(pt.shape[0]):
        pf = pt[g].astype(jnp.float32)
        delta = jnp.sum(pf * dp[g], axis=0, keepdims=True)
        ds_ref[g] = (pf * ((dp[g] - delta) * scaling)).astype(jnp.bfloat16)


def put_dq(ds, kt, turned, dq):
    for h in range(kt.shape[0]):
        turned[h] = dot_nn(kt[h], ds[h // 2, :, pl.ds((h % 2) * TILE, TILE)])
    for h in range(kt.shape[0]):
        dq[:, pl.ds(h * HEAD_DIM, HEAD_DIM)] = turned[h].T.astype(jnp.bfloat16)


def project_pair(dk, dv, wkt, wvt, part):
    return dot_nn(dk[...], wkt[:, part]) + dot_nn(dv[...], wvt[:, part])


def first_out_kernel(last, x, wot, bd):
    @pl.when(lax.axis_index("pipe") == last)
    def _():
        fill_diagonal(bd, wot, x[...], None)


def first_far_kernel(
    last, scaling, bd, qbd, pt, v0, v1, v2, wkt, wvt, far_ref, ds_ref, dk, dv, dp
):
    @pl.when(lax.axis_index("pipe") == last)
    def _():
        own_attention(scaling, bd, pt, v0, v1, v2, dp, ds_ref)
        for g in range(pt.shape[0]):
            cols = pair_cols(g)
            dv[:, cols] = dot_nn(pt[g, 2 * TILE :], bd[g]).astype(jnp.bfloat16)
            dk[:, cols] = dot_nn(ds_ref[g, 2 * TILE :], qbd[g]).astype(jnp.bfloat16)
        far_ref[...] = project_pair(dk, dv, wkt, wvt, slice(None)).astype(jnp.bfloat16)


def first_near_kernel(last, ds_ref, bd, qbd, pt, wkt, wvt, near_ref, dk, dv):
    @pl.when(lax.axis_index("pipe") == last)
    def _():
        for g in range(pt.shape[0]):
            cols = pair_cols(g)
            dv[:, cols] = dot_nn(pt[g, TILE : 2 * TILE], bd[g]).astype(jnp.bfloat16)
            dk[:, cols] = dot_nn(ds_ref[g, TILE : 2 * TILE], qbd[g]).astype(jnp.bfloat16)
        near_ref[...] = project_pair(dk, dv, wkt, wvt, slice(None)).astype(jnp.bfloat16)


def first_own_kernel(
    last, x, ds_ref, bd, qbd, pt, kt, wqt, wkt, wvt, after, base_ref, dq, dk, dv, turned
):
    @pl.when(lax.axis_index("pipe") == last)
    def _():
        for g in range(pt.shape[0]):
            cols = pair_cols(g)
            dv[:, cols] = dot_nn(pt[g, :TILE], bd[g]).astype(jnp.bfloat16)
            dk[:, cols] = dot_nn(ds_ref[g, :TILE], qbd[g]).astype(jnp.bfloat16)
        put_dq(ds_ref, kt, turned, dq)
        base = project_pair(dk, dv, wkt, wvt, slice(None)) + dot_nn(dq[...], wqt[...])
        base_ref[...] = base + x[...].astype(jnp.float32)


def first_sum_kernel(base, near, far, after, suma_ref, sumb_ref):
    total = base[...] + near[...].astype(jnp.float32) + inside(far[...]).astype(jnp.float32)
    total = total.astype(jnp.bfloat16)
    split = suma_ref.shape[1]
    suma_ref[...] = total[:, :split]
    sumb_ref[...] = total[:, split:]


def halo_attention(scaling, bd, po, v, both, ds_ref):
    for g in range(po.shape[0]):
        values = jnp.concatenate([v[:, pair_cols(g)], po[g, TILE : 2 * TILE]], axis=0)
        both[g] = dot_nt(values, bd[g])
    row = lax.broadcasted_iota(jnp.int32, (TILE, 2 * TILE), 0)
    col = lax.broadcasted_iota(jnp.int32, (TILE, 2 * TILE), 1)
    same = (row == col) | (row + TILE == col)
    for g in range(po.shape[0]):
        delta = jnp.sum(jnp.where(same, both[g, TILE:], 0.0), axis=0, keepdims=True)
        ds = po[g, :TILE].astype(jnp.float32) * ((both[g, :TILE] - delta) * scaling)
        ds_ref[g] = ds.astype(jnp.bfloat16)


def own_kernel(
    column,
    scaling,
    acc,
    xa,
    xb,
    wot,
    qbd,
    pt,
    kt,
    v0,
    v1,
    v2,
    wqt,
    dq,
    dk_ref,
    dv_ref,
    base_ref,
    bd,
    dp,
    ds,
    turned,
):
    @pl.when(lax.axis_index("pipe") == column)
    def _():
        fill_diagonal(bd, wot, xb[...], acc)
        own_attention(scaling, bd, pt, v0, v1, v2, dp, ds)
        for g in range(pt.shape[0]):
            cols = pair_cols(g)
            dv_ref[:, cols] = dot_nn(pt[g, :TILE], bd[g])
            dk_ref[:, cols] = dot_nn(ds[g, :TILE], qbd[g])
        put_dq(ds, kt, turned, dq)
        base_ref[...] = xa[...].astype(jnp.float32) + dot_nn(dq[...], wqt[:, : xa.shape[1]])


def near_kernel(
    column,
    scaling,
    xfa,
    xa,
    xb,
    wot,
    qbd,
    po,
    v,
    dk_in,
    dv_in,
    after,
    acc_ref,
    dk_ref,
    dv_ref,
    bd,
    both,
    ds,
):
    @pl.when(lax.axis_index("pipe") == column)
    def _():
        x = jnp.concatenate([xa[...], xb[...]], axis=1)
        fill_diagonal(bd, wot, x, None)
        halo_attention(scaling, bd, po, v, both, ds)
        for g in range(po.shape[0]):
            cols = pair_cols(g)
            dv_ref[:, cols] = dv_in[:, cols] + dot_nn(po[g, :TILE], bd[g])
            dk_ref[:, cols] = dk_in[:, cols] + dot_nn(ds[g], qbd[g])
        acc_ref[...] = dot_nn(inside(xfa[...]), wot[: xfa.shape[1], :])


def far_kernel(
    column,
    scaling,
    acc,
    xb,
    wot,
    qbd,
    po,
    v,
    dk_in,
    dv_in,
    base,
    wkt,
    wvt,
    sum_ref,
    dk_ref,
    dv_ref,
    bd,
    both,
    ds,
):
    @pl.when(lax.axis_index("pipe") == column)
    def _():
        fill_diagonal(bd, wot, inside(xb[...]), acc)
        halo_attention(scaling, bd, po, v, both, ds)
        for g in range(po.shape[0]):
            cols = pair_cols(g)
            dv = dv_in[:, cols] + dot_nn(po[g, :TILE], bd[g])
            dk = dk_in[:, cols] + dot_nn(ds[g], qbd[g])
            dv_ref[:, cols] = dv.astype(jnp.bfloat16)
            dk_ref[:, cols] = dk.astype(jnp.bfloat16)
        part = pl.ds(0, sum_ref.shape[1])
        total = base[...] + project_pair(dk_ref, dv_ref, wkt, wvt, part)
        sum_ref[...] = total.astype(jnp.bfloat16)


def last_columns(dk, dv, dq, own_x, wqt, wkt, wvt):
    rest = own_x.shape[1]
    part = pl.ds(wqt.shape[1] - rest, rest)
    total = own_x[...].astype(jnp.float32) + dot_nn(dq[...], wqt[:, part])
    total = total + project_pair(dk, dv, wkt, wvt, part)
    return total.astype(jnp.bfloat16)


def rest_kernel(column, dk, dv, dq, own_x, wqt, wkt, wvt, sum_ref):
    @pl.when(lax.axis_index("pipe") == column)
    def _():
        sum_ref[...] = last_columns(dk, dv, dq, own_x, wqt, wkt, wvt)


def finish_kernel(dk, dv, dq, own_x, wqt, wkt, wvt, *refs):
    done_refs, out_ref = refs[:-1], refs[-1]
    position = lax.axis_index("pipe")
    split = done_refs[0].shape[1]
    out_ref[:, :split] = done_refs[-1][...]
    out_ref[:, split:] = last_columns(dk, dv, dq, own_x, wqt, wkt, wvt)
    count = len(done_refs) // 2
    for step in range(count):

        @pl.when(position == count - step)
        def _():
            out_ref[:, :split] = done_refs[2 * step][...]
            out_ref[:, split:] = done_refs[2 * step + 1][...]


def body(
    query_rows,
    key_rows,
    value_rows,
    query_weight,
    key_weight,
    value_weight,
    out_weight,
    upstream,
    window,
):
    sections = lax.axis_size("pipe")
    seq_size = lax.axis_size("seq")
    rows, width = query_rows.shape[1:]
    model = out_weight.shape[2]
    split = model // 2
    heads = width // HEAD_DIM
    pairs = heads // 2
    scaling = HEAD_DIM ** (-0.5)
    near_pairs = [(i, i ^ 1) for i in range(seq_size)]
    far_pairs = [(i, i + 1) for i in range(1, seq_size - 1, 2)]
    far_pairs = far_pairs + [(j, i) for i, j in far_pairs]

    def near(value):
        return lax.ppermute(value, "seq", near_pairs)

    def spread(pairs_of):
        tiles = range(seq_size)
        return [
            (c * seq_size + i, d * seq_size + j)
            for c in range(sections)
            for i in tiles
            for d, j in [pairs_of(c, i)]
        ]

    def far(value):
        partner = dict(far_pairs)

        def pairs_of(c, i):
            return (c, partner[i]) if i in partner else ((c + sections // 2) % sections, i)

        return lax.ppermute(value, ("pipe", "seq"), spread(pairs_of))

    def far_within(value, columns):
        moves = [(c * seq_size + i, c * seq_size + j) for c in columns for i, j in far_pairs]
        return lax.ppermute(value, ("pipe", "seq"), moves)

    def hop(value, source):
        def pairs_of(c, i):
            return (2 * source - 1 - c) % sections, i

        return lax.ppermute(value, ("pipe", "seq"), spread(pairs_of))

    vmem = pl.BlockSpec(memory_space=pltpu.VMEM)
    anywhere = pl.BlockSpec(memory_space=pl.ANY)
    bf16, f32 = jnp.bfloat16, jnp.float32
    weight = pltpu.VMEM((model, width), bf16)
    block = (pairs, 2 * TILE, 2 * HEAD_DIM)
    tile = pltpu.VMEM((rows, width), bf16)
    wide = pltpu.VMEM((rows, width), f32)
    whole = jax.ShapeDtypeStruct((rows, model), bf16)
    piece_a = jax.ShapeDtypeStruct((rows, split), bf16)
    piece_b = jax.ShapeDtypeStruct((rows, model - split), bf16)
    dp_scratch = pltpu.VMEM((pairs, 3 * TILE, 2 * TILE), f32)
    turned_scratch = pltpu.VMEM((heads, HEAD_DIM, TILE), f32)
    halo_scratch = [
        pltpu.VMEM(block, bf16),
        pltpu.VMEM(block, f32),
        pltpu.VMEM((pairs, TILE, 2 * TILE), bf16),
    ]
    diagonal = pltpu.VMEM(block, bf16)

    def call(kernel, name, ins, outs, scratch=(), limit=12, cost=0):
        single = not isinstance(outs, list)
        estimate = pl.CostEstimate(flops=cost, bytes_accessed=0, transcendentals=0)
        return pl.pallas_call(
            kernel,
            in_specs=ins,
            out_specs=vmem if single else [vmem] * len(outs),
            out_shape=outs,
            scratch_shapes=list(scratch),
            compiler_params=pltpu.CompilerParams(vmem_limit_bytes=limit * MIB),
            cost_estimate=estimate if cost else None,
            name=name,
        )

    def mark(*values, cost=10**10):
        token = pltpu.VMEM((8, 128), f32)
        return call(mark_kernel, "mark", [anywhere] * len(values), token, cost=cost)(*values)

    k2 = far(key_rows[0])
    v2 = far(value_rows[0])
    k1 = near(key_rows[0])
    wot, wkt, wvt, wqt, q, k, v, x, qbd, keep = call(
        prep_kernel,
        "prep",
        [anywhere] * 9,
        [
            weight,
            weight,
            weight,
            weight,
            tile,
            tile,
            tile,
            tile,
            diagonal,
            pltpu.VMEM((2, pairs, 8, 2 * TILE), jnp.int32),
        ],
        [
            pltpu.VMEM((4, model, width), bf16),
            pltpu.SMEM((window.shape[0], 2, heads), jnp.int32),
            pltpu.SemaphoreType.DMA((21,)),
        ],
        36,
    )(
        out_weight[0],
        key_weight[0],
        value_weight[0],
        query_weight[0],
        query_rows[0],
        key_rows[0],
        value_rows[0],
        upstream,
        jnp.transpose(window, (0, 2, 1)),
    )
    v1 = near(v)

    def clean(value, *before):
        ins = [vmem] + [anywhere] * len(before)
        return call(clean_kernel, "clean", ins, tile, cost=10**10)(value, *before)

    pt, kt = call(
        functools.partial(prob_kernel, scaling),
        "prob",
        [vmem] * 5,
        [
            pltpu.VMEM((pairs, 3 * TILE, 2 * rows), bf16),
            pltpu.VMEM((heads, HEAD_DIM, 3 * TILE), bf16),
        ],
        [dp_scratch],
    )(keep, qbd, k, k1, clean(k2, k1))

    bd = call(
        functools.partial(first_out_kernel, sections - 1), "first_out", [vmem] * 2, diagonal
    )(x, wot)
    v2 = clean(v2, pt, bd)
    to_far, ds = call(
        functools.partial(first_far_kernel, sections - 1, scaling),
        "first_far",
        [vmem] * 8,
        [whole, pltpu.VMEM((pairs, 3 * TILE, 2 * rows), bf16)],
        [tile, tile, dp_scratch],
    )(bd, qbd, pt, v, v1, v2, wkt, wvt)
    from_far = far(to_far)
    to_near = call(
        functools.partial(first_near_kernel, sections - 1), "first_near", [vmem] * 6, whole, [tile, tile])(
        ds, bd, qbd, pt, wkt, wvt
    )
    from_near = near(to_near)
    packet = pltpu.VMEM((pairs, 3 * TILE, 2 * HEAD_DIM), bf16)
    po_to_near, po_to_far = call(
        functools.partial(out_kernel, sections - 1),
        "out",
        [vmem] * 5 + [anywhere],
        [packet, packet],
    )(pt, q, v, v1, v2, to_near)
    pof = far_within(po_to_far, range(sections - 1))
    pon = near(po_to_near)
    turn = call(turn_kernel, "turn", [vmem], diagonal)
    qbdn, qbdf = turn(pon), turn(pof)
    base = call(
        functools.partial(first_own_kernel, sections - 1),
        "first_own",
        [vmem] * 9 + [anywhere],
        wide,
        [tile, tile, tile, turned_scratch],
    )(x, ds, bd, qbd, pt, kt, wqt, wkt, wvt, po_to_far)
    done_a, done_b = call(
        first_sum_kernel, "first_sum", [vmem] * 3 + [anywhere], [piece_a, piece_b]
    )(base, from_near, from_far, mark(from_far))
    done = [done_a, done_b]

    for step in range(1, sections):
        source = sections - step
        xa = hop(done_a, source)
        xb = hop(done_b, source)
        acc, xa_copy = call(
            functools.partial(begin_kernel, source - 1), "begin", [vmem] * 2 + [anywhere], [wide, piece_a]
        )(xa, wot, qbdn)
        xfa, xfb = far(xa_copy), far(xb)
        xna, xnb = near(xa_copy), near(xb)
        dq, dk, dv, base = call(
            functools.partial(own_kernel, source - 1, scaling),
            "own",
            [vmem] * 11,
            [tile, wide, wide, pltpu.VMEM((rows, split), f32)],
            [
                pltpu.VMEM(block, bf16),
                dp_scratch,
                pltpu.VMEM((pairs, 3 * TILE, 2 * TILE), bf16),
                turned_scratch,
            ],
        )(acc, xa, xb, wot, qbd, pt, kt, v, v1, v2, wqt)
        acc, dk, dv = call(
            functools.partial(near_kernel, source - 1, scaling),
            "near",
            [vmem] * 9 + [anywhere],
            [wide, wide, wide],
            halo_scratch,
        )(xfa, xna, xnb, wot, qbdn, pon, v, dk, dv, mark(xfa, xna, cost=10**8))
        done_a, dk, dv = call(
            functools.partial(far_kernel, source - 1, scaling),
            "far",
            [vmem] * 11,
            [piece_a, tile, tile],
            halo_scratch,
        )(acc, xfb, wot, qbdf, pof, v, dk, dv, base, wkt, wvt)
        rest_in = (dk, dv, dq, xb, wqt, wkt, wvt)
        if step < sections - 1:
            done_b = call(
                functools.partial(rest_kernel, source - 1), "rest", [vmem] * 7, piece_b
            )(*rest_in)
            done += [done_a, done_b]
    out = call(
        finish_kernel,
        "finish",
        [vmem] * (8 + len(done)),
        jax.ShapeDtypeStruct((rows, model), bf16),
    )(*rest_in, *done, done_a)
    return out[None]


def solution(mesh):
    in_specs = (
        P("pipe", "seq", None),
        P("pipe", "seq", None),
        P("pipe", "seq", None),
        P("pipe", None, None),
        P("pipe", None, None),
        P("pipe", None, None),
        P("pipe", None, None),
        P("seq", None),
        P(),
    )
    out_specs = P("pipe", "seq", None)
    return jax.shard_map(body, mesh=mesh, in_specs=in_specs, out_specs=out_specs, check_vma=False)
```

```python
import functools

import jax
import jax.numpy as jnp
from jax import lax
from jax.experimental import pallas as pl
from jax.experimental.pallas import tpu as pltpu
from jax.sharding import PartitionSpec as P

HEAD_DIM = 128
TILE = 128
MIB = 1 << 20


def dot_nt(a, b):
    return lax.dot_general(a, b, (((1,), (1,)), ((), ())), preferred_element_type=jnp.float32)


def dot_nn(a, b):
    return lax.dot_general(a, b, (((1,), (0,)), ((), ())), preferred_element_type=jnp.float32)


def pair_cols(g):
    return pl.ds(g * 2 * HEAD_DIM, 2 * HEAD_DIM)


def put_diagonal(target, g, value):
    target[g, pl.ds(0, TILE), pl.ds(0, HEAD_DIM)] = value[:, :HEAD_DIM]
    target[g, pl.ds(TILE, TILE), pl.ds(HEAD_DIM, HEAD_DIM)] = value[:, HEAD_DIM:]


def prep_kernel(
    last,
    wo_hbm,
    wk_hbm,
    wv_hbm,
    wq_hbm,
    q_hbm,
    k_hbm,
    v_hbm,
    x_hbm,
    window,
    wot,
    wkt,
    wvt,
    wqt,
    q,
    k,
    v,
    x,
    qbd,
    keep,
    bd,
    raw,
    flags,
    sems,
):
    groups = 4
    rows = raw.shape[1] // groups
    small = [
        pltpu.make_async_copy(src, dst, sems.at[n])
        for n, (src, dst) in enumerate(((q_hbm, q), (k_hbm, k), (v_hbm, v), (x_hbm, x)))
    ]
    sources = (wo_hbm, wk_hbm, wv_hbm, wq_hbm)

    def large(n, g):
        part = pl.ds(g * rows, rows)
        return pltpu.make_async_copy(
            sources[n].at[part], raw.at[n, part], sems.at[4 + n * groups + g]
        )

    window_copy = pltpu.make_async_copy(window, flags, sems.at[20])
    window_copy.start()
    for copy in small:
        copy.start()
    for n in range(len(sources)):
        for g in range(groups):
            large(n, g).start()
    qbd[...] = jnp.zeros_like(qbd)
    for copy in small:
        copy.wait()
    for g in range(qbd.shape[0]):
        put_diagonal(qbd, g, q[:, pair_cols(g)])
    for n, dst in enumerate((wot, wkt, wvt, wqt)):

        @pl.loop(0, groups)
        def _(g, n=n, dst=dst):
            start = pl.multiple_of(g * rows, rows)
            large(n, g).wait()
            for r in range(0, rows, TILE):
                part = pl.ds(start + r, TILE)
                dst[:, part] = raw[n, part, :].T

        if n == 0:

            @pl.when(lax.axis_index("pipe") == last)
            def _():
                fill_diagonal(bd, wot, x[...], None)
    window_copy.wait()
    tile = lax.axis_index("seq")
    odd = lax.rem(tile, 2)
    lane = lax.broadcasted_iota(jnp.int32, keep.shape[2:], 1)
    for b, side in enumerate((1 - odd, odd)):
        for g in range(keep.shape[1]):
            keep[b, g] = jnp.where(
                lane < TILE, flags[tile, side, 2 * g], flags[tile, side, 2 * g + 1]
            )


def prob_kernel(scaling, keep, qbd, k0, k1, k2, pt_ref, kt_ref, scores):
    pairs = pt_ref.shape[0]
    for g in range(pairs):
        cols = pair_cols(g)
        keys = jnp.concatenate([k0[:, cols], k1[:, cols], k2[:, cols]], axis=0)
        scores[g] = dot_nt(keys, qbd[g])
        for b, k_ref in enumerate((k0, k1, k2)):
            for n in range(2):
                h = 2 * g + n
                part = k_ref[:, pl.ds(h * HEAD_DIM, HEAD_DIM)]
                kt_ref[h, :, pl.ds(b * TILE, TILE)] = part.T
    for g in range(pairs):
        parts = []
        for b in range(3):
            s = scaling * scores[g, pl.ds(b * TILE, TILE)]
            if b > 0:
                s = jnp.where(keep[b - 1, g, 0:1] > 0, s, -jnp.inf)
            parts.append(s)
        top = jnp.maximum(jnp.maximum(parts[0], parts[1]), parts[2])
        top = jnp.max(top, axis=0, keepdims=True)
        weights = [jnp.exp(s - top) for s in parts]
        total = jnp.sum(weights[0] + weights[1] + weights[2], axis=0, keepdims=True)
        scale = 1.0 / total
        for b, w in enumerate(weights):
            pt_ref[g, pl.ds(b * TILE, TILE), :] = (w * scale).astype(jnp.bfloat16)


def out_kernel(last, pt, q, v0, v1, v2, after, pon_ref, pof_ref):
    @pl.when(lax.axis_index("pipe") < last)
    def _():
        for g in range(pt.shape[0]):
            pon_ref[g, :TILE] = pt[g, TILE : 2 * TILE]
            pof_ref[g, :TILE] = pt[g, 2 * TILE :]
            for n in range(2):
                cols = pl.ds((2 * g + n) * HEAD_DIM, HEAD_DIM)
                lanes = pl.ds(n * HEAD_DIM, HEAD_DIM)
                values = jnp.concatenate([v0[:, cols], v1[:, cols], v2[:, cols]], axis=0)
                out = dot_nn(pt[g, :, lanes].T, values).astype(jnp.bfloat16)
                pon_ref[g, pl.ds(TILE, TILE), lanes] = out
                pof_ref[g, pl.ds(TILE, TILE), lanes] = out
            queries = q[:, pair_cols(g)]
            pon_ref[g, 2 * TILE :] = queries
            pof_ref[g, 2 * TILE :] = queries


def turn_kernel(po, qbd):
    qbd[...] = jnp.zeros_like(qbd)
    for g in range(qbd.shape[0]):
        put_diagonal(qbd, g, po[g, 2 * TILE :])


def inside(value):
    tile = lax.axis_index("seq")
    edge = (tile == 0) | (tile == lax.axis_size("seq") - 1)
    return jnp.where(edge, jnp.zeros_like(value), value)


def clean_kernel(value, *refs):
    refs[-1][...] = inside(value[...])


def mark_kernel(*refs):
    refs[-1][...] = jnp.zeros_like(refs[-1])


def begin_kernel(column, xa_ref, wot, after, acc_ref, copy_ref):
    @pl.when(lax.axis_index("pipe") == column)
    def _():
        x = xa_ref[...]
        copy_ref[...] = x
        acc_ref[...] = dot_nn(x, wot[: x.shape[1], :])


def fill_diagonal(bd, wot, x, acc_ref):
    bd[...] = jnp.zeros_like(bd)
    start = wot.shape[0] - x.shape[1]
    for g in range(bd.shape[0]):
        cols = pair_cols(g)
        d_out = dot_nn(x, wot[start:, cols])
        if acc_ref is not None:
            d_out = acc_ref[:, cols] + d_out
        put_diagonal(bd, g, d_out.astype(jnp.bfloat16))


def own_attention(scaling, bd, pt, v0, v1, v2, dp, ds_ref):
    for g in range(pt.shape[0]):
        cols = pair_cols(g)
        values = jnp.concatenate([v0[:, cols], v1[:, cols], v2[:, cols]], axis=0)
        dp[g] = dot_nt(values, bd[g])
    for g in range(pt.shape[0]):
        pf = pt[g].astype(jnp.float32)
        delta = jnp.sum(pf * dp[g], axis=0, keepdims=True)
        ds_ref[g] = (pf * ((dp[g] - delta) * scaling)).astype(jnp.bfloat16)


def put_dq(ds, kt, turned, dq):
    for h in range(kt.shape[0]):
        turned[h] = dot_nn(kt[h], ds[h // 2, :, pl.ds((h % 2) * TILE, TILE)])
    for h in range(kt.shape[0]):
        dq[:, pl.ds(h * HEAD_DIM, HEAD_DIM)] = turned[h].T.astype(jnp.bfloat16)


def project_pair(dk, dv, wkt, wvt, part):
    return dot_nn(dk[...], wkt[:, part]) + dot_nn(dv[...], wvt[:, part])


def first_far_kernel(
    last, scaling, bd, qbd, pt, v0, v1, v2, wkt, wvt, far_ref, ds_ref, dk, dv, dp
):
    @pl.when(lax.axis_index("pipe") == last)
    def _():
        own_attention(scaling, bd, pt, v0, v1, v2, dp, ds_ref)
        for g in range(pt.shape[0]):
            cols = pair_cols(g)
            dv[:, cols] = dot_nn(pt[g, 2 * TILE :], bd[g]).astype(jnp.bfloat16)
            dk[:, cols] = dot_nn(ds_ref[g, 2 * TILE :], qbd[g]).astype(jnp.bfloat16)
        far_ref[...] = project_pair(dk, dv, wkt, wvt, slice(None)).astype(jnp.bfloat16)


def first_near_kernel(last, ds_ref, bd, qbd, pt, wkt, wvt, near_ref, dk, dv):
    @pl.when(lax.axis_index("pipe") == last)
    def _():
        for g in range(pt.shape[0]):
            cols = pair_cols(g)
            dv[:, cols] = dot_nn(pt[g, TILE : 2 * TILE], bd[g]).astype(jnp.bfloat16)
            dk[:, cols] = dot_nn(ds_ref[g, TILE : 2 * TILE], qbd[g]).astype(jnp.bfloat16)
        near_ref[...] = project_pair(dk, dv, wkt, wvt, slice(None)).astype(jnp.bfloat16)


def first_own_kernel(
    last, x, ds_ref, bd, qbd, pt, kt, wqt, wkt, wvt, after, base_ref, dq, dk, dv, turned
):
    @pl.when(lax.axis_index("pipe") == last)
    def _():
        for g in range(pt.shape[0]):
            cols = pair_cols(g)
            dv[:, cols] = dot_nn(pt[g, :TILE], bd[g]).astype(jnp.bfloat16)
            dk[:, cols] = dot_nn(ds_ref[g, :TILE], qbd[g]).astype(jnp.bfloat16)
        put_dq(ds_ref, kt, turned, dq)
        base = project_pair(dk, dv, wkt, wvt, slice(None)) + dot_nn(dq[...], wqt[...])
        base_ref[...] = base + x[...].astype(jnp.float32)


def first_sum_kernel(base, near, far, after, suma_ref, sumb_ref):
    total = base[...] + near[...].astype(jnp.float32) + inside(far[...]).astype(jnp.float32)
    total = total.astype(jnp.bfloat16)
    split = suma_ref.shape[1]
    suma_ref[...] = total[:, :split]
    sumb_ref[...] = total[:, split:]


def halo_attention(scaling, bd, po, v, both, ds_ref):
    for g in range(po.shape[0]):
        values = jnp.concatenate([v[:, pair_cols(g)], po[g, TILE : 2 * TILE]], axis=0)
        both[g] = dot_nt(values, bd[g])
    row = lax.broadcasted_iota(jnp.int32, (TILE, 2 * TILE), 0)
    col = lax.broadcasted_iota(jnp.int32, (TILE, 2 * TILE), 1)
    same = (row == col) | (row + TILE == col)
    for g in range(po.shape[0]):
        delta = jnp.sum(jnp.where(same, both[g, TILE:], 0.0), axis=0, keepdims=True)
        ds = po[g, :TILE].astype(jnp.float32) * ((both[g, :TILE] - delta) * scaling)
        ds_ref[g] = ds.astype(jnp.bfloat16)


def own_kernel(
    column,
    scaling,
    acc,
    xa,
    xb,
    wot,
    qbd,
    pt,
    kt,
    v0,
    v1,
    v2,
    wqt,
    dq,
    dk_ref,
    dv_ref,
    base_ref,
    bd,
    dp,
    ds,
    turned,
):
    @pl.when(lax.axis_index("pipe") == column)
    def _():
        fill_diagonal(bd, wot, xb[...], acc)
        own_attention(scaling, bd, pt, v0, v1, v2, dp, ds)
        for g in range(pt.shape[0]):
            cols = pair_cols(g)
            dv_ref[:, cols] = dot_nn(pt[g, :TILE], bd[g])
            dk_ref[:, cols] = dot_nn(ds[g, :TILE], qbd[g])
        put_dq(ds, kt, turned, dq)
        base_ref[...] = xa[...].astype(jnp.float32) + dot_nn(dq[...], wqt[:, : xa.shape[1]])


def near_kernel(
    column,
    scaling,
    xfa,
    xa,
    xb,
    wot,
    qbd,
    po,
    v,
    dk_in,
    dv_in,
    after,
    acc_ref,
    dk_ref,
    dv_ref,
    bd,
    both,
    ds,
):
    @pl.when(lax.axis_index("pipe") == column)
    def _():
        x = jnp.concatenate([xa[...], xb[...]], axis=1)
        fill_diagonal(bd, wot, x, None)
        halo_attention(scaling, bd, po, v, both, ds)
        for g in range(po.shape[0]):
            cols = pair_cols(g)
            dv_ref[:, cols] = dv_in[:, cols] + dot_nn(po[g, :TILE], bd[g])
            dk_ref[:, cols] = dk_in[:, cols] + dot_nn(ds[g], qbd[g])
        acc_ref[...] = dot_nn(inside(xfa[...]), wot[: xfa.shape[1], :])


def far_kernel(
    column,
    scaling,
    acc,
    xb,
    wot,
    qbd,
    po,
    v,
    dk_in,
    dv_in,
    base,
    wkt,
    wvt,
    sum_ref,
    dk_ref,
    dv_ref,
    bd,
    both,
    ds,
):
    @pl.when(lax.axis_index("pipe") == column)
    def _():
        fill_diagonal(bd, wot, inside(xb[...]), acc)
        halo_attention(scaling, bd, po, v, both, ds)
        for g in range(po.shape[0]):
            cols = pair_cols(g)
            dv = dv_in[:, cols] + dot_nn(po[g, :TILE], bd[g])
            dk = dk_in[:, cols] + dot_nn(ds[g], qbd[g])
            dv_ref[:, cols] = dv.astype(jnp.bfloat16)
            dk_ref[:, cols] = dk.astype(jnp.bfloat16)
        part = pl.ds(0, sum_ref.shape[1])
        total = base[...] + project_pair(dk_ref, dv_ref, wkt, wvt, part)
        sum_ref[...] = total.astype(jnp.bfloat16)


def last_columns(dk, dv, dq, own_x, wqt, wkt, wvt):
    rest = own_x.shape[1]
    part = pl.ds(wqt.shape[1] - rest, rest)
    total = own_x[...].astype(jnp.float32) + dot_nn(dq[...], wqt[:, part])
    total = total + project_pair(dk, dv, wkt, wvt, part)
    return total.astype(jnp.bfloat16)


def rest_kernel(column, dk, dv, dq, own_x, wqt, wkt, wvt, sum_ref):
    @pl.when(lax.axis_index("pipe") == column)
    def _():
        sum_ref[...] = last_columns(dk, dv, dq, own_x, wqt, wkt, wvt)


def finish_kernel(dk, dv, dq, own_x, wqt, wkt, wvt, *refs):
    done_refs, (out_ref, tail, sems) = refs[:-3], refs[-3:]
    position = lax.axis_index("pipe")
    split = done_refs[0].shape[1]
    count = len(done_refs) // 2

    def write(n, value):
        part = pl.ds(n * split, value.shape[1])
        return pltpu.make_async_copy(value, out_ref.at[:, part], sems.at[n])

    @pl.when(position == 0)
    def _():
        write(0, done_refs[-1]).start()
        tail[...] = last_columns(dk, dv, dq, own_x, wqt, wkt, wvt)
        write(1, tail).start()
        write(0, done_refs[-1]).wait()
        write(1, tail).wait()

    for step in range(count):

        @pl.when(position == count - step)
        def _():
            copies = [write(0, done_refs[2 * step]), write(1, done_refs[2 * step + 1])]
            for copy in copies:
                copy.start()
            for copy in copies:
                copy.wait()


def body(
    query_rows,
    key_rows,
    value_rows,
    query_weight,
    key_weight,
    value_weight,
    out_weight,
    upstream,
    window,
):
    sections = lax.axis_size("pipe")
    seq_size = lax.axis_size("seq")
    rows, width = query_rows.shape[1:]
    model = out_weight.shape[2]
    split = model // 2
    heads = width // HEAD_DIM
    pairs = heads // 2
    scaling = HEAD_DIM ** (-0.5)
    near_pairs = [(i, i ^ 1) for i in range(seq_size)]
    far_pairs = [(i, i + 1) for i in range(1, seq_size - 1, 2)]
    far_pairs = far_pairs + [(j, i) for i, j in far_pairs]

    def near(value):
        return lax.ppermute(value, "seq", near_pairs)

    def spread(pairs_of):
        tiles = range(seq_size)
        return [
            (c * seq_size + i, d * seq_size + j)
            for c in range(sections)
            for i in tiles
            for d, j in [pairs_of(c, i)]
        ]

    def far(value):
        partner = dict(far_pairs)

        def pairs_of(c, i):
            return (c, partner[i]) if i in partner else ((c + sections // 2) % sections, i)

        return lax.ppermute(value, ("pipe", "seq"), spread(pairs_of))

    def far_within(value, columns):
        moves = [(c * seq_size + i, c * seq_size + j) for c in columns for i, j in far_pairs]
        return lax.ppermute(value, ("pipe", "seq"), moves)

    def hop(value, source):
        def pairs_of(c, i):
            return (2 * source - 1 - c) % sections, i

        return lax.ppermute(value, ("pipe", "seq"), spread(pairs_of))

    vmem = pl.BlockSpec(memory_space=pltpu.VMEM)
    anywhere = pl.BlockSpec(memory_space=pl.ANY)
    bf16, f32 = jnp.bfloat16, jnp.float32
    weight = pltpu.VMEM((model, width), bf16)
    block = (pairs, 2 * TILE, 2 * HEAD_DIM)
    tile = pltpu.VMEM((rows, width), bf16)
    wide = pltpu.VMEM((rows, width), f32)
    whole = jax.ShapeDtypeStruct((rows, model), bf16)
    piece_a = jax.ShapeDtypeStruct((rows, split), bf16)
    piece_b = jax.ShapeDtypeStruct((rows, model - split), bf16)
    dp_scratch = pltpu.VMEM((pairs, 3 * TILE, 2 * TILE), f32)
    turned_scratch = pltpu.VMEM((heads, HEAD_DIM, TILE), f32)
    halo_scratch = [
        pltpu.VMEM(block, bf16),
        pltpu.VMEM(block, f32),
        pltpu.VMEM((pairs, TILE, 2 * TILE), bf16),
    ]
    diagonal = pltpu.VMEM(block, bf16)

    def call(kernel, name, ins, outs, scratch=(), limit=12, cost=0, place=vmem):
        single = not isinstance(outs, list)
        estimate = pl.CostEstimate(flops=cost, bytes_accessed=0, transcendentals=0)
        return pl.pallas_call(
            kernel,
            in_specs=ins,
            out_specs=place if single else [vmem] * len(outs),
            out_shape=outs,
            scratch_shapes=list(scratch),
            compiler_params=pltpu.CompilerParams(vmem_limit_bytes=limit * MIB),
            cost_estimate=estimate if cost else None,
            name=name,
        )

    def mark(*values, cost=10**10):
        token = pltpu.VMEM((8, 128), f32)
        return call(mark_kernel, "mark", [anywhere] * len(values), token, cost=cost)(*values)

    k2 = far(key_rows[0])
    v2 = far(value_rows[0])
    k1 = near(key_rows[0])
    wot, wkt, wvt, wqt, q, k, v, x, qbd, keep, bd = call(
        functools.partial(prep_kernel, sections - 1),
        "prep",
        [anywhere] * 9,
        [
            weight,
            weight,
            weight,
            weight,
            tile,
            tile,
            tile,
            tile,
            diagonal,
            pltpu.VMEM((2, pairs, 8, 2 * TILE), jnp.int32),
            diagonal,
        ],
        [
            pltpu.VMEM((4, model, width), bf16),
            pltpu.SMEM((window.shape[0], 2, heads), jnp.int32),
            pltpu.SemaphoreType.DMA((21,)),
        ],
        36,
    )(
        out_weight[0],
        key_weight[0],
        value_weight[0],
        query_weight[0],
        query_rows[0],
        key_rows[0],
        value_rows[0],
        upstream,
        jnp.transpose(window, (0, 2, 1)),
    )
    v1 = near(v)

    def clean(value, *before):
        ins = [vmem] + [anywhere] * len(before)
        return call(clean_kernel, "clean", ins, tile, cost=10**10)(value, *before)

    pt, kt = call(
        functools.partial(prob_kernel, scaling),
        "prob",
        [vmem] * 5,
        [
            pltpu.VMEM((pairs, 3 * TILE, 2 * rows), bf16),
            pltpu.VMEM((heads, HEAD_DIM, 3 * TILE), bf16),
        ],
        [dp_scratch],
    )(keep, qbd, k, k1, clean(k2, k1))

    v2 = clean(v2, pt)
    to_far, ds = call(
        functools.partial(first_far_kernel, sections - 1, scaling),
        "first_far",
        [vmem] * 8,
        [whole, pltpu.VMEM((pairs, 3 * TILE, 2 * rows), bf16)],
        [tile, tile, dp_scratch],
    )(bd, qbd, pt, v, v1, v2, wkt, wvt)
    from_far = far(to_far)
    to_near = call(
        functools.partial(first_near_kernel, sections - 1), "first_near", [vmem] * 6, whole, [tile, tile])(
        ds, bd, qbd, pt, wkt, wvt
    )
    from_near = near(to_near)
    packet = pltpu.VMEM((pairs, 3 * TILE, 2 * HEAD_DIM), bf16)
    po_to_near, po_to_far = call(
        functools.partial(out_kernel, sections - 1),
        "out",
        [vmem] * 5 + [anywhere],
        [packet, packet],
    )(pt, q, v, v1, v2, to_near)
    pof = far_within(po_to_far, range(sections - 1))
    pon = near(po_to_near)
    turn = call(turn_kernel, "turn", [vmem], diagonal)
    qbdn, qbdf = turn(pon), turn(pof)
    base = call(
        functools.partial(first_own_kernel, sections - 1),
        "first_own",
        [vmem] * 9 + [anywhere],
        wide,
        [tile, tile, tile, turned_scratch],
    )(x, ds, bd, qbd, pt, kt, wqt, wkt, wvt, po_to_far)
    done_a, done_b = call(
        first_sum_kernel, "first_sum", [vmem] * 3 + [anywhere], [piece_a, piece_b]
    )(base, from_near, from_far, mark(from_far))
    done = [done_a, done_b]

    for step in range(1, sections):
        source = sections - step
        xa = hop(done_a, source)
        xb = hop(done_b, source)
        acc, xa_copy = call(
            functools.partial(begin_kernel, source - 1), "begin", [vmem] * 2 + [anywhere], [wide, piece_a]
        )(xa, wot, qbdn)
        xfa, xfb = far(xa_copy), far(xb)
        xna, xnb = near(xa_copy), near(xb)
        dq, dk, dv, base = call(
            functools.partial(own_kernel, source - 1, scaling),
            "own",
            [vmem] * 11,
            [tile, wide, wide, pltpu.VMEM((rows, split), f32)],
            [
                pltpu.VMEM(block, bf16),
                dp_scratch,
                pltpu.VMEM((pairs, 3 * TILE, 2 * TILE), bf16),
                turned_scratch,
            ],
        )(acc, xa, xb, wot, qbd, pt, kt, v, v1, v2, wqt)
        acc, dk, dv = call(
            functools.partial(near_kernel, source - 1, scaling),
            "near",
            [vmem] * 9 + [anywhere],
            [wide, wide, wide],
            halo_scratch,
        )(xfa, xna, xnb, wot, qbdn, pon, v, dk, dv, mark(xfa, xna, cost=10**8))
        done_a, dk, dv = call(
            functools.partial(far_kernel, source - 1, scaling),
            "far",
            [vmem] * 11,
            [piece_a, tile, tile],
            halo_scratch,
        )(acc, xfb, wot, qbdf, pof, v, dk, dv, base, wkt, wvt)
        rest_in = (dk, dv, dq, xb, wqt, wkt, wvt)
        if step < sections - 1:
            done_b = call(
                functools.partial(rest_kernel, source - 1), "rest", [vmem] * 7, piece_b
            )(*rest_in)
            done += [done_a, done_b]
    out = call(
        finish_kernel,
        "finish",
        [vmem] * (8 + len(done)),
        jax.ShapeDtypeStruct((rows, model), bf16),
        [pltpu.VMEM((rows, model - split), bf16), pltpu.SemaphoreType.DMA((2,))],
        place=anywhere,
    )(*rest_in, *done, done_a)
    return out[None]


def solution(mesh):
    in_specs = (
        P("pipe", "seq", None),
        P("pipe", "seq", None),
        P("pipe", "seq", None),
        P("pipe", None, None),
        P("pipe", None, None),
        P("pipe", None, None),
        P("pipe", None, None),
        P("seq", None),
        P(),
    )
    out_specs = P("pipe", "seq", None)
    return jax.shard_map(body, mesh=mesh, in_specs=in_specs, out_specs=out_specs, check_vma=False)
```

```python
import functools

import jax
import jax.numpy as jnp
from jax import lax
from jax.experimental import pallas as pl
from jax.experimental.pallas import tpu as pltpu
from jax.sharding import PartitionSpec as P

HEAD_DIM = 128
TILE = 128
MIB = 1 << 20


def dot_nt(a, b):
    return lax.dot_general(a, b, (((1,), (1,)), ((), ())), preferred_element_type=jnp.float32)


def dot_nn(a, b):
    return lax.dot_general(a, b, (((1,), (0,)), ((), ())), preferred_element_type=jnp.float32)


def pair_cols(g):
    return pl.ds(g * 2 * HEAD_DIM, 2 * HEAD_DIM)


def put_diagonal(target, g, value):
    target[g, pl.ds(0, TILE), pl.ds(0, HEAD_DIM)] = value[:, :HEAD_DIM]
    target[g, pl.ds(TILE, TILE), pl.ds(HEAD_DIM, HEAD_DIM)] = value[:, HEAD_DIM:]


def prep_kernel(
    last,
    wo_hbm,
    wk_hbm,
    wv_hbm,
    wq_hbm,
    q_hbm,
    k_hbm,
    v_hbm,
    x_hbm,
    window,
    wot,
    wkt,
    wvt,
    wqt,
    q,
    k,
    v,
    x,
    qbd,
    keep,
    bd,
    raw,
    flags,
    sems,
):
    groups = 4
    rows = raw.shape[1] // groups
    small = [
        pltpu.make_async_copy(src, dst, sems.at[n])
        for n, (src, dst) in enumerate(((q_hbm, q), (k_hbm, k), (v_hbm, v), (x_hbm, x)))
    ]
    sources = (wo_hbm, wk_hbm, wv_hbm, wq_hbm)

    def large(n, g):
        part = pl.ds(g * rows, rows)
        return pltpu.make_async_copy(
            sources[n].at[part], raw.at[n, part], sems.at[4 + n * groups + g]
        )

    window_copy = pltpu.make_async_copy(window, flags, sems.at[20])
    window_copy.start()
    for copy in small:
        copy.start()
    for n in range(len(sources)):
        for g in range(groups):
            large(n, g).start()
    qbd[...] = jnp.zeros_like(qbd)
    for copy in small:
        copy.wait()
    for g in range(qbd.shape[0]):
        put_diagonal(qbd, g, q[:, pair_cols(g)])
    for n, dst in enumerate((wot, wkt, wvt, wqt)):

        @pl.loop(0, groups)
        def _(g, n=n, dst=dst):
            start = pl.multiple_of(g * rows, rows)
            large(n, g).wait()
            for r in range(0, rows, TILE):
                part = pl.ds(start + r, TILE)
                dst[:, part] = raw[n, part, :].T

        if n == 0:

            @pl.when(lax.axis_index("pipe") == last)
            def _():
                fill_diagonal(bd, wot, x[...], None)
    window_copy.wait()
    tile = lax.axis_index("seq")
    odd = lax.rem(tile, 2)
    lane = lax.broadcasted_iota(jnp.int32, keep.shape[2:], 1)
    for b, side in enumerate((1 - odd, odd)):
        for g in range(keep.shape[1]):
            keep[b, g] = jnp.where(
                lane < TILE, flags[tile, side, 2 * g], flags[tile, side, 2 * g + 1]
            )


def prob_kernel(scaling, keep, qbd, k0, k1, k2, pt_ref, kt_ref, scores):
    pairs = pt_ref.shape[0]
    for g in range(pairs):
        cols = pair_cols(g)
        keys = jnp.concatenate([k0[:, cols], k1[:, cols], k2[:, cols]], axis=0)
        scores[g] = dot_nt(keys, qbd[g])
        for b, k_ref in enumerate((k0, k1, k2)):
            for n in range(2):
                h = 2 * g + n
                part = k_ref[:, pl.ds(h * HEAD_DIM, HEAD_DIM)]
                kt_ref[h, :, pl.ds(b * TILE, TILE)] = part.T
    for g in range(pairs):
        parts = []
        for b in range(3):
            s = scaling * scores[g, pl.ds(b * TILE, TILE)]
            if b > 0:
                s = jnp.where(keep[b - 1, g, 0:1] > 0, s, -jnp.inf)
            parts.append(s)
        top = jnp.maximum(jnp.maximum(parts[0], parts[1]), parts[2])
        top = jnp.max(top, axis=0, keepdims=True)
        weights = [jnp.exp(s - top) for s in parts]
        total = jnp.sum(weights[0] + weights[1] + weights[2], axis=0, keepdims=True)
        scale = 1.0 / total
        for b, w in enumerate(weights):
            pt_ref[g, pl.ds(b * TILE, TILE), :] = (w * scale).astype(jnp.bfloat16)


def out_kernel(last, pt, q, v0, v1, v2, after, pon_ref, pof_ref):
    @pl.when(lax.axis_index("pipe") < last)
    def _():
        for g in range(pt.shape[0]):
            pon_ref[g, :TILE] = pt[g, TILE : 2 * TILE]
            pof_ref[g, :TILE] = pt[g, 2 * TILE :]
            for n in range(2):
                cols = pl.ds((2 * g + n) * HEAD_DIM, HEAD_DIM)
                lanes = pl.ds(n * HEAD_DIM, HEAD_DIM)
                values = jnp.concatenate([v0[:, cols], v1[:, cols], v2[:, cols]], axis=0)
                out = dot_nn(pt[g, :, lanes].T, values).astype(jnp.bfloat16)
                pon_ref[g, pl.ds(TILE, TILE), lanes] = out
                pof_ref[g, pl.ds(TILE, TILE), lanes] = out
            queries = q[:, pair_cols(g)]
            pon_ref[g, 2 * TILE :] = queries
            pof_ref[g, 2 * TILE :] = queries


def turn_kernel(po, qbd):
    qbd[...] = jnp.zeros_like(qbd)
    for g in range(qbd.shape[0]):
        put_diagonal(qbd, g, po[g, 2 * TILE :])


def inside(value):
    tile = lax.axis_index("seq")
    edge = (tile == 0) | (tile == lax.axis_size("seq") - 1)
    return jnp.where(edge, jnp.zeros_like(value), value)


def clean_kernel(value, *refs):
    refs[-1][...] = inside(value[...])


def mark_kernel(*refs):
    refs[-1][...] = jnp.zeros_like(refs[-1])


def begin_kernel(column, xa_ref, wot, after, acc_ref, copy_ref):
    @pl.when(lax.axis_index("pipe") == column)
    def _():
        x = xa_ref[...]
        copy_ref[...] = x
        acc_ref[...] = dot_nn(x, wot[: x.shape[1], :])


def fill_diagonal(bd, wot, x, acc_ref):
    bd[...] = jnp.zeros_like(bd)
    start = wot.shape[0] - x.shape[1]
    for g in range(bd.shape[0]):
        cols = pair_cols(g)
        d_out = dot_nn(x, wot[start:, cols])
        if acc_ref is not None:
            d_out = acc_ref[:, cols] + d_out
        put_diagonal(bd, g, d_out.astype(jnp.bfloat16))


def own_attention(scaling, bd, pt, v0, v1, v2, dp, ds_ref):
    for g in range(pt.shape[0]):
        cols = pair_cols(g)
        values = jnp.concatenate([v0[:, cols], v1[:, cols], v2[:, cols]], axis=0)
        dp[g] = dot_nt(values, bd[g])
    for g in range(pt.shape[0]):
        pf = pt[g].astype(jnp.float32)
        delta = jnp.sum(pf * dp[g], axis=0, keepdims=True)
        ds_ref[g] = (pf * ((dp[g] - delta) * scaling)).astype(jnp.bfloat16)


def put_dq(ds, kt, turned, dq):
    for h in range(kt.shape[0]):
        turned[h] = dot_nn(kt[h], ds[h // 2, :, pl.ds((h % 2) * TILE, TILE)])
    for h in range(kt.shape[0]):
        dq[:, pl.ds(h * HEAD_DIM, HEAD_DIM)] = turned[h].T.astype(jnp.bfloat16)


def project_pair(dk, dv, wkt, wvt, part):
    return dot_nn(dk[...], wkt[:, part]) + dot_nn(dv[...], wvt[:, part])


def first_far_kernel(
    last, scaling, bd, qbd, pt, v0, v1, v2, wkt, wvt, far_ref, ds_ref, dk, dv, dp
):
    @pl.when(lax.axis_index("pipe") == last)
    def _():
        own_attention(scaling, bd, pt, v0, v1, v2, dp, ds_ref)
        for g in range(pt.shape[0]):
            cols = pair_cols(g)
            dv[:, cols] = dot_nn(pt[g, 2 * TILE :], bd[g]).astype(jnp.bfloat16)
            dk[:, cols] = dot_nn(ds_ref[g, 2 * TILE :], qbd[g]).astype(jnp.bfloat16)
        far_ref[...] = project_pair(dk, dv, wkt, wvt, slice(None)).astype(jnp.bfloat16)


def first_near_kernel(last, ds_ref, bd, qbd, pt, wkt, wvt, near_ref, dk, dv):
    @pl.when(lax.axis_index("pipe") == last)
    def _():
        for g in range(pt.shape[0]):
            cols = pair_cols(g)
            dv[:, cols] = dot_nn(pt[g, TILE : 2 * TILE], bd[g]).astype(jnp.bfloat16)
            dk[:, cols] = dot_nn(ds_ref[g, TILE : 2 * TILE], qbd[g]).astype(jnp.bfloat16)
        near_ref[...] = project_pair(dk, dv, wkt, wvt, slice(None)).astype(jnp.bfloat16)


def first_own_kernel(
    last, x, ds_ref, bd, qbd, pt, kt, wqt, wkt, wvt, after, base_ref, dq, dk, dv, turned
):
    @pl.when(lax.axis_index("pipe") == last)
    def _():
        for g in range(pt.shape[0]):
            cols = pair_cols(g)
            dv[:, cols] = dot_nn(pt[g, :TILE], bd[g]).astype(jnp.bfloat16)
            dk[:, cols] = dot_nn(ds_ref[g, :TILE], qbd[g]).astype(jnp.bfloat16)
        put_dq(ds_ref, kt, turned, dq)
        base = project_pair(dk, dv, wkt, wvt, slice(None)) + dot_nn(dq[...], wqt[...])
        base_ref[...] = base + x[...].astype(jnp.float32)


def first_sum_kernel(base, near, far, after, suma_ref, sumb_ref):
    total = base[...] + near[...].astype(jnp.float32) + inside(far[...]).astype(jnp.float32)
    total = total.astype(jnp.bfloat16)
    split = suma_ref.shape[1]
    suma_ref[...] = total[:, :split]
    sumb_ref[...] = total[:, split:]


def halo_attention(scaling, bd, po, v, both, ds_ref):
    for g in range(po.shape[0]):
        values = jnp.concatenate([v[:, pair_cols(g)], po[g, TILE : 2 * TILE]], axis=0)
        both[g] = dot_nt(values, bd[g])
    row = lax.broadcasted_iota(jnp.int32, (TILE, 2 * TILE), 0)
    col = lax.broadcasted_iota(jnp.int32, (TILE, 2 * TILE), 1)
    same = (row == col) | (row + TILE == col)
    for g in range(po.shape[0]):
        delta = jnp.sum(jnp.where(same, both[g, TILE:], 0.0), axis=0, keepdims=True)
        ds = po[g, :TILE].astype(jnp.float32) * ((both[g, :TILE] - delta) * scaling)
        ds_ref[g] = ds.astype(jnp.bfloat16)


def own_kernel(
    column,
    scaling,
    acc,
    xa,
    xb,
    wot,
    qbd,
    pt,
    kt,
    v0,
    v1,
    v2,
    wqt,
    dq,
    dk_ref,
    dv_ref,
    base_ref,
    bd,
    dp,
    ds,
    turned,
):
    @pl.when(lax.axis_index("pipe") == column)
    def _():
        fill_diagonal(bd, wot, xb[...], acc)
        own_attention(scaling, bd, pt, v0, v1, v2, dp, ds)
        for g in range(pt.shape[0]):
            cols = pair_cols(g)
            dv_ref[:, cols] = dot_nn(pt[g, :TILE], bd[g])
            dk_ref[:, cols] = dot_nn(ds[g, :TILE], qbd[g])
        put_dq(ds, kt, turned, dq)
        base_ref[...] = xa[...].astype(jnp.float32) + dot_nn(dq[...], wqt[:, : xa.shape[1]])


def near_kernel(
    column,
    scaling,
    xfa,
    xa,
    xb,
    wot,
    qbd,
    po,
    v,
    dk_in,
    dv_in,
    after,
    acc_ref,
    dk_ref,
    dv_ref,
    bd,
    both,
    ds,
):
    @pl.when(lax.axis_index("pipe") == column)
    def _():
        x = jnp.concatenate([xa[...], xb[...]], axis=1)
        fill_diagonal(bd, wot, x, None)
        halo_attention(scaling, bd, po, v, both, ds)
        for g in range(po.shape[0]):
            cols = pair_cols(g)
            dv_ref[:, cols] = dv_in[:, cols] + dot_nn(po[g, :TILE], bd[g])
            dk_ref[:, cols] = dk_in[:, cols] + dot_nn(ds[g], qbd[g])
        acc_ref[...] = dot_nn(inside(xfa[...]), wot[: xfa.shape[1], :])


def far_kernel(
    column,
    scaling,
    acc,
    xb,
    wot,
    qbd,
    po,
    v,
    dk_in,
    dv_in,
    base,
    wkt,
    wvt,
    sum_ref,
    dk_ref,
    dv_ref,
    bd,
    both,
    ds,
):
    @pl.when(lax.axis_index("pipe") == column)
    def _():
        fill_diagonal(bd, wot, inside(xb[...]), acc)
        halo_attention(scaling, bd, po, v, both, ds)
        for g in range(po.shape[0]):
            cols = pair_cols(g)
            dv = dv_in[:, cols] + dot_nn(po[g, :TILE], bd[g])
            dk = dk_in[:, cols] + dot_nn(ds[g], qbd[g])
            dv_ref[:, cols] = dv.astype(jnp.bfloat16)
            dk_ref[:, cols] = dk.astype(jnp.bfloat16)
        part = pl.ds(0, sum_ref.shape[1])
        total = base[...] + project_pair(dk_ref, dv_ref, wkt, wvt, part)
        sum_ref[...] = total.astype(jnp.bfloat16)


def last_columns(dk, dv, dq, own_x, wqt, wkt, wvt):
    rest = own_x.shape[1]
    part = pl.ds(wqt.shape[1] - rest, rest)
    total = own_x[...].astype(jnp.float32) + dot_nn(dq[...], wqt[:, part])
    total = total + project_pair(dk, dv, wkt, wvt, part)
    return total.astype(jnp.bfloat16)


def rest_kernel(column, dk, dv, dq, own_x, wqt, wkt, wvt, sum_ref):
    @pl.when(lax.axis_index("pipe") == column)
    def _():
        sum_ref[...] = last_columns(dk, dv, dq, own_x, wqt, wkt, wvt)


def finish_kernel(dk, dv, dq, own_x, wqt, wkt, wvt, *refs):
    done_refs, out_ref = refs[:-1], refs[-1]
    position = lax.axis_index("pipe")
    split = done_refs[0].shape[1]
    out_ref[:, :split] = done_refs[-1][...]
    out_ref[:, split:] = last_columns(dk, dv, dq, own_x, wqt, wkt, wvt)
    count = len(done_refs) // 2
    for step in range(count):

        @pl.when(position == count - step)
        def _():
            out_ref[:, :split] = done_refs[2 * step][...]
            out_ref[:, split:] = done_refs[2 * step + 1][...]


def body(
    query_rows,
    key_rows,
    value_rows,
    query_weight,
    key_weight,
    value_weight,
    out_weight,
    upstream,
    window,
):
    sections = lax.axis_size("pipe")
    seq_size = lax.axis_size("seq")
    rows, width = query_rows.shape[1:]
    model = out_weight.shape[2]
    split = model // 2
    heads = width // HEAD_DIM
    pairs = heads // 2
    scaling = HEAD_DIM ** (-0.5)
    near_pairs = [(i, i ^ 1) for i in range(seq_size)]
    far_pairs = [(i, i + 1) for i in range(1, seq_size - 1, 2)]
    far_pairs = far_pairs + [(j, i) for i, j in far_pairs]

    def near(value):
        return lax.ppermute(value, "seq", near_pairs)

    def spread(pairs_of):
        tiles = range(seq_size)
        return [
            (c * seq_size + i, d * seq_size + j)
            for c in range(sections)
            for i in tiles
            for d, j in [pairs_of(c, i)]
        ]

    def far(value):
        partner = dict(far_pairs)

        def pairs_of(c, i):
            return (c, partner[i]) if i in partner else ((c + sections // 2) % sections, i)

        return lax.ppermute(value, ("pipe", "seq"), spread(pairs_of))

    def far_within(value, columns):
        moves = [(c * seq_size + i, c * seq_size + j) for c in columns for i, j in far_pairs]
        return lax.ppermute(value, ("pipe", "seq"), moves)

    def hop(value, source):
        def pairs_of(c, i):
            return (2 * source - 1 - c) % sections, i

        return lax.ppermute(value, ("pipe", "seq"), spread(pairs_of))

    vmem = pl.BlockSpec(memory_space=pltpu.VMEM)
    anywhere = pl.BlockSpec(memory_space=pl.ANY)
    bf16, f32 = jnp.bfloat16, jnp.float32
    weight = pltpu.VMEM((model, width), bf16)
    block = (pairs, 2 * TILE, 2 * HEAD_DIM)
    tile = pltpu.VMEM((rows, width), bf16)
    wide = pltpu.VMEM((rows, width), f32)
    whole = jax.ShapeDtypeStruct((rows, model), bf16)
    piece_a = jax.ShapeDtypeStruct((rows, split), bf16)
    piece_b = jax.ShapeDtypeStruct((rows, model - split), bf16)
    dp_scratch = pltpu.VMEM((pairs, 3 * TILE, 2 * TILE), f32)
    turned_scratch = pltpu.VMEM((heads, HEAD_DIM, TILE), f32)
    halo_scratch = [
        pltpu.VMEM(block, bf16),
        pltpu.VMEM(block, f32),
        pltpu.VMEM((pairs, TILE, 2 * TILE), bf16),
    ]
    diagonal = pltpu.VMEM(block, bf16)

    def call(kernel, name, ins, outs, scratch=(), limit=12, cost=0):
        single = not isinstance(outs, list)
        estimate = pl.CostEstimate(flops=cost, bytes_accessed=0, transcendentals=0)
        return pl.pallas_call(
            kernel,
            in_specs=ins,
            out_specs=vmem if single else [vmem] * len(outs),
            out_shape=outs,
            scratch_shapes=list(scratch),
            compiler_params=pltpu.CompilerParams(vmem_limit_bytes=limit * MIB),
            cost_estimate=estimate if cost else None,
            name=name,
        )

    def mark(*values, cost=10**10):
        token = pltpu.VMEM((8, 128), f32)
        return call(mark_kernel, "mark", [anywhere] * len(values), token, cost=cost)(*values)

    k2 = far(key_rows[0])
    v2 = far(value_rows[0])
    k1 = near(key_rows[0])
    wot, wkt, wvt, wqt, q, k, v, x, qbd, keep, bd = call(
        functools.partial(prep_kernel, sections - 1),
        "prep",
        [anywhere] * 9,
        [
            weight,
            weight,
            weight,
            weight,
            tile,
            tile,
            tile,
            tile,
            diagonal,
            pltpu.VMEM((2, pairs, 8, 2 * TILE), jnp.int32),
            diagonal,
        ],
        [
            pltpu.VMEM((4, model, width), bf16),
            pltpu.SMEM((window.shape[0], 2, heads), jnp.int32),
            pltpu.SemaphoreType.DMA((21,)),
        ],
        36,
    )(
        out_weight[0],
        key_weight[0],
        value_weight[0],
        query_weight[0],
        query_rows[0],
        key_rows[0],
        value_rows[0],
        upstream,
        jnp.transpose(window, (0, 2, 1)),
    )
    v1 = near(v)

    def clean(value, *before):
        ins = [vmem] + [anywhere] * len(before)
        return call(clean_kernel, "clean", ins, tile, cost=10**10)(value, *before)

    pt, kt = call(
        functools.partial(prob_kernel, scaling),
        "prob",
        [vmem] * 5,
        [
            pltpu.VMEM((pairs, 3 * TILE, 2 * rows), bf16),
            pltpu.VMEM((heads, HEAD_DIM, 3 * TILE), bf16),
        ],
        [dp_scratch],
    )(keep, qbd, k, k1, clean(k2, k1))

    v2 = clean(v2, pt)
    to_far, ds = call(
        functools.partial(first_far_kernel, sections - 1, scaling),
        "first_far",
        [vmem] * 8,
        [whole, pltpu.VMEM((pairs, 3 * TILE, 2 * rows), bf16)],
        [tile, tile, dp_scratch],
    )(bd, qbd, pt, v, v1, v2, wkt, wvt)
    from_far = far(to_far)
    to_near = call(
        functools.partial(first_near_kernel, sections - 1), "first_near", [vmem] * 6, whole, [tile, tile])(
        ds, bd, qbd, pt, wkt, wvt
    )
    from_near = near(to_near)
    packet = pltpu.VMEM((pairs, 3 * TILE, 2 * HEAD_DIM), bf16)
    po_to_near, po_to_far = call(
        functools.partial(out_kernel, sections - 1),
        "out",
        [vmem] * 5 + [anywhere],
        [packet, packet],
    )(pt, q, v, v1, v2, to_near)
    pof = far_within(po_to_far, range(sections - 1))
    pon = near(po_to_near)
    turn = call(turn_kernel, "turn", [vmem], diagonal)
    qbdn, qbdf = turn(pon), turn(pof)
    base = call(
        functools.partial(first_own_kernel, sections - 1),
        "first_own",
        [vmem] * 9 + [anywhere],
        wide,
        [tile, tile, tile, turned_scratch],
    )(x, ds, bd, qbd, pt, kt, wqt, wkt, wvt, po_to_far)
    done_a, done_b = call(
        first_sum_kernel, "first_sum", [vmem] * 3 + [anywhere], [piece_a, piece_b]
    )(base, from_near, from_far, mark(from_far))
    done = [done_a, done_b]

    for step in range(1, sections):
        source = sections - step
        xa = hop(done_a, source)
        xb = hop(done_b, source)
        acc, xa_copy = call(
            functools.partial(begin_kernel, source - 1), "begin", [vmem] * 2 + [anywhere], [wide, piece_a]
        )(xa, wot, qbdn)
        xfa, xfb = far(xa_copy), far(xb)
        xna, xnb = near(xa_copy), near(xb)
        dq, dk, dv, base = call(
            functools.partial(own_kernel, source - 1, scaling),
            "own",
            [vmem] * 11,
            [tile, wide, wide, pltpu.VMEM((rows, split), f32)],
            [
                pltpu.VMEM(block, bf16),
                dp_scratch,
                pltpu.VMEM((pairs, 3 * TILE, 2 * TILE), bf16),
                turned_scratch,
            ],
        )(acc, xa, xb, wot, qbd, pt, kt, v, v1, v2, wqt)
        acc, dk, dv = call(
            functools.partial(near_kernel, source - 1, scaling),
            "near",
            [vmem] * 9 + [anywhere],
            [wide, wide, wide],
            halo_scratch,
        )(xfa, xna, xnb, wot, qbdn, pon, v, dk, dv, mark(xfa, xna, cost=10**8))
        done_a, dk, dv = call(
            functools.partial(far_kernel, source - 1, scaling),
            "far",
            [vmem] * 11,
            [piece_a, tile, tile],
            halo_scratch,
        )(acc, xfb, wot, qbdf, pof, v, dk, dv, base, wkt, wvt)
        rest_in = (dk, dv, dq, xb, wqt, wkt, wvt)
        if step < sections - 1:
            done_b = call(
                functools.partial(rest_kernel, source - 1), "rest", [vmem] * 7, piece_b
            )(*rest_in)
            done += [done_a, done_b]
    out = call(
        finish_kernel,
        "finish",
        [vmem] * (8 + len(done)),
        jax.ShapeDtypeStruct((rows, model), bf16),
    )(*rest_in, *done, done_a)
    return out[None]


def solution(mesh):
    in_specs = (
        P("pipe", "seq", None),
        P("pipe", "seq", None),
        P("pipe", "seq", None),
        P("pipe", None, None),
        P("pipe", None, None),
        P("pipe", None, None),
        P("pipe", None, None),
        P("seq", None),
        P(),
    )
    out_specs = P("pipe", "seq", None)
    return jax.shard_map(body, mesh=mesh, in_specs=in_specs, out_specs=out_specs, check_vma=False)
```
